32 devices in a mesh: slab: 4 (over z), grp: 8 (over y, x, core).
Axes of the slice: x: 2, y: 2, z: 4, core: 2. Of those that a mesh axis runs over, the one named last changes fastest.
Arguments:
- samples: float32 [32768, 6, 128], P(('slab', 'grp')), as said below
- block_ids: int32 [32768], P(('slab', 'grp')), may hold values from 0 to 32767, as said below
- tile_counts: int32 [32768], P(('slab', 'grp')), may hold values from 0 to 128
- occupied: int32 [8, 16, 256], P('slab', 'grp'), may hold values 0 or 1
- coupling: float32 [27, 64, 64], replicated, may hold values from -0.06 to 0.06
Outputs:
- solution_field: float32 [64, 8, 16, 256], P(None, 'slab', 'grp')
- residual: float32 [64, 8, 16, 256], P(None, 'slab', 'grp')
The draws below stay inside these ranges and needn't reach their ends.
Inputs may be any that keep to these rules, and one draw needn't show every extreme that they name: `samples`: the first three components of every sample lie in [0, 1). `block_ids`: slot j * 32 + c of a device's slots (c below 32) carries a block whose x // 2 is the slab index and y // 2 the grp index of the device of linear index j over slab then grp; ids number blocks as (x * 16 + y) * 256 + z; every block is named by exactly one slot over all devices.
All inputs are finite; a program needn't handle non-finite values. No bound on the sum of `occupied` on one device may be relied on, other than what follows from the above.
Results may differ from the reference program's by a relative error of at most 0.0003.
Values sent between devices are 32-bit elements; how exact they have to be, the bound alone decides.
A program may use at most 128 MiB of HBM per device.

```python
import jax
import jax.numpy as jnp
from jax import lax

NODES = 64
TILE = 128
BX = 2
BY = 2
BZ = 256
ITERS = 3
GX = 8
GY = 16
CAP = 32
SLOTS = 32768
N_SLAB = 4
N_GRP = 8


def draw_samples(key, part):
    key_pos, key_dir = jax.random.split(key, 2)
    position = jax.random.uniform(key_pos, (SLOTS, 3, TILE), jnp.float32, 0.0, 0.999)
    normals = jnp.clip(jax.random.normal(key_dir, (SLOTS, 3, TILE), jnp.float32), -4.0, 4.0)
    return jnp.concatenate([position, normals], axis=1)


def draw_block_ids(key, part):
    per_slab = GY // BY
    devs = GX // BX * per_slab
    blocks = BX * BY * BZ
    keys = jax.random.split(key, devs)
    orders = jax.vmap(lambda single: jax.random.permutation(single, blocks))(keys).astype(jnp.int32)
    position = jnp.arange(SLOTS, dtype=jnp.int32)
    source = position // (CAP * devs)
    target = position // CAP % devs
    lane = position % CAP
    local = orders[target, source * CAP + lane]
    block_x = target // per_slab * BX + local // (BY * BZ)
    block_y = target % per_slab * BY + local // BZ % BY
    block_z = local % BZ
    return (block_x * GY + block_y) * BZ + block_z


def draw_tile_counts(key, part):
    raw = jax.random.randint(key, (SLOTS,), 0, 2 * TILE, jnp.int32)
    counts = jnp.minimum(raw, TILE)
    return counts.at[0].set(TILE).at[SLOTS - 1].set(0)


def place_ends(result, rng, least, largest):
    extent = result.shape
    spot = [jax.random.randint(jax.random.fold_in(rng, axis), (), 0, extent[axis]) for axis in range(len(extent))]
    result = result.at[tuple(spot)].set(least)
    longest = extent.index(max(extent))
    spot[longest] = (spot[longest] + 1) % extent[longest]
    return result.at[tuple(spot)].set(largest)


def scatter_about(stream_key, extent, spread, reach, kind=jnp.bfloat16):
    return jnp.clip(spread * jax.random.normal(stream_key, extent, jnp.float32), -reach, reach).astype(kind)


def setup_inputs(seed: int = 0) -> dict:
    seeds = jax.random.split(jax.random.key(seed), 6)
    samples = draw_samples(jax.random.fold_in(seeds[5], 71), 0)
    block_ids = draw_block_ids(jax.random.fold_in(seeds[5], 71), 0)
    tile_counts = draw_tile_counts(jax.random.fold_in(seeds[5], 71), 0)
    occupied = place_ends((jax.random.randint(seeds[3], (GX, GY, BZ), 0, 10) < 7).astype(jnp.int32), jax.random.fold_in(seeds[3], 1), 0, 1)
    coupling = scatter_about(seeds[4], (27, NODES, NODES), 0.01, 0.06, jnp.float32)
    return {"samples": samples, "block_ids": block_ids, "tile_counts": tile_counts, "occupied": occupied, "coupling": coupling}


HIGH = lax.Precision.HIGHEST


def bspline_value(diff):
    mag = jnp.abs(diff)
    return jnp.where(mag < 0.5, 0.75 - mag * mag, jnp.where(mag < 1.5, 0.5 * (1.5 - mag) ** 2, 0.0))


def bspline_slope(diff):
    mag = jnp.abs(diff)
    outer = -(1.5 - mag) * diff / jnp.maximum(mag, 0.5)
    return jnp.where(mag < 0.5, -2.0 * diff, jnp.where(mag < 1.5, outer, 0.0))


def splat_tiles(tile_data, counts):
    slots = tile_data.shape[0]
    width = tile_data.shape[2]
    lanes = jnp.arange(width, dtype=jnp.int32)[None, :]
    valid = (lanes < counts[:, None]).astype(jnp.float32)
    centres = jnp.arange(4, dtype=jnp.float32) + 0.5
    diff = 4.0 * tile_data[:, 0:3, :][:, :, None, :] - centres[None, None, :, None]
    values = bspline_value(diff)
    slopes = 4.0 * bspline_slope(diff)
    normals = tile_data[:, 3:6, :] * valid[:, None, :]
    pair_val = (values[:, 1][:, :, None, :] * values[:, 2][:, None, :, :]).reshape(slots, 16, width)
    pair_dy = (slopes[:, 1][:, :, None, :] * values[:, 2][:, None, :, :]).reshape(slots, 16, width)
    pair_dz = (values[:, 1][:, :, None, :] * slopes[:, 2][:, None, :, :]).reshape(slots, 16, width)
    term_x = jnp.einsum('tis,tks->tik', slopes[:, 0] * normals[:, 0][:, None, :], pair_val, precision=HIGH)
    term_y = jnp.einsum('tis,tks->tik', values[:, 0] * normals[:, 1][:, None, :], pair_dy, precision=HIGH)
    term_z = jnp.einsum('tis,tks->tik', values[:, 0] * normals[:, 2][:, None, :], pair_dz, precision=HIGH)
    dens = jnp.einsum('tis,tks->tik', values[:, 0] * valid[:, None, :], pair_val, precision=HIGH)
    rhs = (term_x + term_y + term_z).reshape(slots, 64)
    return jnp.concatenate([rhs, dens.reshape(slots, 64)], axis=1)


def symmetric_blocks(coupling):
    coupled = 0.5 * (coupling + jnp.transpose(jnp.flip(coupling, 0), (0, 2, 1)))
    rowabs = jnp.sum(jnp.abs(coupled), axis=(0, 2))
    return coupled, rowabs


def apply_stiffness(field, padded, coupled, diag, mask):
    nodes, size_x, size_y, size_z = field.shape
    total = jnp.zeros((nodes, size_x * size_y * size_z), jnp.float32)
    for offset in range(27):
        shift_x = offset // 9
        shift_y = offset // 3 % 3
        shift_z = offset % 3
        piece = padded[:, shift_x:shift_x + size_x, shift_y:shift_y + size_y, shift_z:shift_z + size_z]
        total = total + jnp.dot(coupled[offset], piece.reshape(nodes, -1), precision=HIGH)
    return diag * field - mask * total.reshape(field.shape)


def reference(samples, block_ids, tile_counts, occupied, coupling):
    devs = N_SLAB * N_GRP
    grouped = samples.reshape(devs, SLOTS // devs, 6, TILE)
    grouped_counts = tile_counts.reshape(devs, SLOTS // devs)
    contrib = lax.map(lambda pair: splat_tiles(pair[0], pair[1]), (grouped, grouped_counts))
    contrib = contrib.reshape(SLOTS, 128)
    summed = jax.ops.segment_sum(contrib, block_ids, num_segments=GX * GY * BZ)
    grid = summed.T.reshape(2, 64, GX, GY, BZ)
    right_side = grid[0]
    density = grid[1]
    coupled, rowabs = symmetric_blocks(coupling)
    diag = rowabs[:, None, None, None] + 0.5 + 4.0 * density
    mask = occupied.astype(jnp.float32)[None]

    def operate(field):
        padded = jnp.pad(field * mask, ((0, 0), (1, 1), (1, 1), (1, 1)))
        return apply_stiffness(field, padded, coupled, diag, mask)

    solution_field = jnp.zeros_like(right_side)
    residual = right_side
    direction = right_side
    norm_now = jnp.sum(residual * residual)
    for step in range(ITERS):
        image = operate(direction)
        alpha = norm_now / jnp.sum(direction * image)
        solution_field = solution_field + alpha * direction
        residual = residual - alpha * image
        norm_next = jnp.sum(residual * residual)
        direction = residual + (norm_next / norm_now) * direction
        norm_now = norm_next
    return solution_field, residual
```

```python
import functools

import jax
import jax.numpy as jnp
from jax import lax
from jax.experimental import pallas as pl
from jax.experimental.pallas import tpu as pltpu
from jax.sharding import PartitionSpec as P

ITERS = 3
MESH = pl.DeviceIdType.MESH
F32 = jnp.float32
BF16 = jnp.bfloat16


def hats(u):
    hat, low = [], []
    for j in range(5):
        g = u - float(j)
        h = jnp.maximum(1.0 - jnp.abs(g), 0.0)
        hat.append(h)
        low.append((0.5 + 0.5 * g) * h)
    values = [low[i] + (hat[i + 1] - low[i + 1]) for i in range(4)]
    slopes = [hat[i] - hat[i + 1] for i in range(4)]
    return values, slopes


def split(x):
    hi = x.astype(BF16)
    return hi, (x - hi.astype(F32)).astype(BF16)


def total(x):
    return jnp.sum(jnp.sum(x, axis=0, keepdims=True), axis=1, keepdims=True)


def kernel(n_slab, n_grp, samples, counts, idrows, occupied, coupling, x_out, r_out,
           fac, nodes, send, recv, cs, chi, clo, diag, halo_out, halo_in, image, res, wvec,
           zvec, dvec, qvec, zq, part, parts, weights, a2a_send, a2a_recv, halo_send, halo_recv,
           sum_send, sum_recv):
    devs = n_slab * n_grp
    cap = send.shape[1] - 8
    per = 128 // cap
    groups = samples.shape[0] // 128
    slab = lax.axis_index("slab")
    grp = lax.axis_index("grp")
    me = slab * n_grp + grp

    part[...] = jnp.zeros_like(part)
    barrier = pltpu.get_barrier_semaphore()

    def greet(k, carry):
        other = lax.rem(me + k, devs)
        pl.semaphore_signal(barrier, inc=1, device_id=(other // n_grp, lax.rem(other, n_grp)),
                            device_id_type=MESH)
        return carry

    lax.fori_loop(1, devs, greet, 0)
    pl.semaphore_wait(barrier, devs - 1)

    def splat(step, carry):
        g = lax.rem(me // per + groups // 2 + step, groups)
        rows = pl.ds(pl.multiple_of(g * 128, 128), 128)
        live = lax.broadcasted_iota(jnp.int32, (128, 128), 0) < counts[g]
        for d in range(3):
            values, slopes = hats(4.0 * samples[rows, d, :].T)
            normal = 4.0 * samples[rows, 3 + d, :].T
            if d == 0:
                normal = jnp.where(live, normal, 0.0)
            for i in range(4):
                fac[8 * d + i] = jnp.where(live, values[i], 0.0) if d == 0 else values[i]
                fac[8 * d + 4 + i] = slopes[i] * normal

        def pair(k, carry):
            j = k // 2
            first = lax.rem(k, 2) * 2

            def add(s, accs):
                at = pl.ds(pl.multiple_of(s * 8, 8), 8)
                v0 = [fac[i, at, :] for i in range(4)]
                s0 = [fac[4 + i, at, :] for i in range(4)]
                v1 = fac[8 + j, at, :]
                s1 = fac[12 + j, at, :]
                out = []
                for e in range(2):
                    v2 = fac[16 + first + e, at, :]
                    s2 = fac[20 + first + e, at, :]
                    p = v1 * v2
                    q = s1 * v2 + v1 * s2
                    for i in range(4):
                        out.append(accs[len(out)] + (s0[i] * p + v0[i] * q))
                    for i in range(4):
                        out.append(accs[len(out)] + v0[i] * p)
                return tuple(out)

            zero = jnp.zeros((8, 128), F32)
            accs = lax.fori_loop(0, 16, add, (zero,) * 16, unroll=True)
            for e in range(2):
                for i in range(8):
                    row = 16 * i + 4 * j + first + e
                    nodes[pl.ds(row, 1), :] = jnp.sum(accs[8 * e + i], axis=0, keepdims=True)
            return carry

        lax.fori_loop(0, 8, pair, 0)
        tiles = nodes[...].T
        for c in range(per):
            target = g * per + c
            send[target, 0:cap, :] = tiles[c * cap:(c + 1) * cap]
            send[target, cap:cap + 8, :] = jnp.broadcast_to(idrows[target], (8, 128))

            @pl.when(target != me)
            def _():
                pltpu.make_async_remote_copy(
                    src_ref=send.at[target], dst_ref=recv.at[me],
                    send_sem=a2a_send, recv_sem=a2a_recv,
                    device_id=(target // n_grp, lax.rem(target, n_grp)), device_id_type=MESH,
                ).start()

            @pl.when(target == me)
            def _():
                recv[target] = send[target]
        return carry

    lax.fori_loop(0, groups, splat, 0)

    rowabs = jnp.zeros((64, 64), F32)
    for k in range(27):
        c = 0.5 * (coupling[k] + coupling[26 - k].T)
        rowabs = rowabs + jnp.abs(c)
        base = (2 - k // 9) * 192 + (2 - k // 3 % 3) * 64
        cs[base:base + 64, (k % 3) * 64:(k % 3) * 64 + 64] = c
    hi, lo = split(cs[...])
    chi[...] = hi
    clo[...] = lo
    rowabs = jnp.sum(rowabs, axis=1, keepdims=True) + 0.5
    mask = [occupied[c].astype(F32) for c in range(4)]

    everyone = pl.ds(0, devs - 1)
    pltpu.make_async_copy(recv.at[everyone], recv.at[everyone], a2a_recv).wait()
    pltpu.make_async_copy(send.at[everyone], send.at[everyone], a2a_send).wait()

    for k in range(groups):
        tiles = recv[k * per:(k + 1) * per, 0:cap, :].reshape(128, 128)
        hi, lo = split(tiles)
        weights[k * 128:(k + 1) * 128, 0:128] = hi
        weights[k * 128:(k + 1) * 128, 128:256] = lo
    ids = []
    for k in range(groups):
        row = recv[k * per, cap:cap + 1, :]
        for c in range(1, per):
            row = row + recv[k * per + c, cap:cap + 1, :]
        ids.append(row)
    ids = jnp.concatenate(ids, axis=1).astype(jnp.int32)
    for c in range(4):
        place = lax.broadcasted_iota(jnp.int32, (256, 1024), 0) + 256 * c
        hot = jnp.where(place == ids, 1.0, 0.0).astype(BF16)
        block = jnp.dot(hot, weights[...], preferred_element_type=F32)
        block = (block[:, 0:128] + block[:, 128:256]).T
        res[c] = block[0:64]
        diag[c] = rowabs + 4.0 * block[64:128]

    lane = lax.broadcasted_iota(jnp.int32, (64, 256), 1)

    def frame(fx, fy, m):
        up = jnp.where(lane == 0, 0.0, pltpu.roll(m, 1, 1))
        down = jnp.where(lane == 255, 0.0, pltpu.roll(m, 255, 1))
        hi, lo = split(jnp.concatenate([up, m, down], axis=0))
        xs = [x for x in range(2) if 0 <= fx - x <= 2]
        ys = [y for y in range(2) if 0 <= fy - y <= 2]
        size = 64 * len(ys)
        starts = [(2 - (fx - x)) * 192 + (2 - (fy - ys[0])) * 64 for x in xs]
        high = [chi[s:s + size, :] for s in starts]
        low = [clo[s:s + size, :] for s in starts]
        rows = size * len(xs)
        first = jnp.dot(jnp.concatenate(high + low, axis=0), hi, preferred_element_type=F32)
        second = jnp.dot(jnp.concatenate(high, axis=0), lo, preferred_element_type=F32)
        sums = first[0:rows] + (first[rows:2 * rows] + second)
        for a, x in enumerate(xs):
            for b, y in enumerate(ys):
                at = a * size + b * 64
                image[2 * x + y] += sums[at:at + 64]

    has = {
        ("x", 0): slab > 0, ("x", 3): slab < n_slab - 1,
        ("y", 0): grp > 0, ("y", 3): grp < n_grp - 1,
    }

    def both(a, b):
        return jnp.logical_and(a, b)

    def send_copy(t, src, f, dev):
        return pltpu.make_async_remote_copy(
            src_ref=src, dst_ref=halo_in.at[t, f], send_sem=halo_send.at[t, f],
            recv_sem=halo_recv.at[t, f], device_id=dev, device_id_type=MESH)

    def apply(t, src, dst):
        for c in range(4):
            halo_out[t, c] = mask[c] * src[c]
            image[c] = jnp.zeros((64, 256), F32)
        sends = []
        for y in (0, 1):
            sends.append((has["x", 3], halo_out.at[t, 2 + y], 0 * 4 + 1 + y, (slab + 1, grp)))
            sends.append((has["x", 0], halo_out.at[t, y], 3 * 4 + 1 + y, (slab - 1, grp)))
        for x in (0, 1):
            sends.append((has["y", 3], halo_out.at[t, 2 * x + 1], (1 + x) * 4, (slab, grp + 1)))
            sends.append((has["y", 0], halo_out.at[t, 2 * x], (1 + x) * 4 + 3, (slab, grp - 1)))
        for cond, ref, f, dev in sends:
            @pl.when(cond)
            def _():
                send_copy(t, ref, f, dev).start()
        for x in (0, 1):
            for y in (0, 1):
                frame(1 + x, 1 + y, halo_out[t, 2 * x + y])
        for fx in (0, 3):
            for y in (1, 0):
                f = fx * 4 + 1 + y
                corner = fx * 4 + (0 if y == 1 else 3)
                dev = (slab, grp + 1) if y == 1 else (slab, grp - 1)
                onward = has["y", 3] if y == 1 else has["y", 0]

                @pl.when(has["x", fx])
                def _():
                    send_copy(t, halo_in.at[t, f], f, (slab, grp)).wait_recv()

                @pl.when(both(has["x", fx], onward))
                def _():
                    send_copy(t, halo_in.at[t, f], corner, dev).start()
                sends.append((both(has["x", fx], onward), halo_in.at[t, f], corner, dev))
        for x in (0, 1):
            for fy in (0, 3):
                f = (1 + x) * 4 + fy

                @pl.when(has["y", fy])
                def _():
                    send_copy(t, halo_in.at[t, f], f, (slab, grp)).wait_recv()
                    frame(1 + x, fy, halo_in[t, f])
        for fx in (0, 3):
            for y in (0, 1):
                @pl.when(has["x", fx])
                def _():
                    frame(fx, 1 + y, halo_in[t, fx * 4 + 1 + y])
        for fx in (0, 3):
            for fy in (0, 3):
                f = fx * 4 + fy

                @pl.when(both(has["x", fx], has["y", fy]))
                def _():
                    send_copy(t, halo_in.at[t, f], f, (slab, grp)).wait_recv()
                    frame(fx, fy, halo_in[t, f])
        for c in range(4):
            dst[c] = diag[c] * src[c] - mask[c] * image[c]
        for cond, ref, f, dev in sends:
            @pl.when(cond)
            def _():
                send_copy(t, ref, f, dev).wait_send()

    def start_sum(t, pairs):
        for k, (a, b) in enumerate(pairs):
            acc = a[0] * b[0]
            for c in range(1, 4):
                acc = acc + a[c] * b[c]
            part[t, k:k + 1, :] = jnp.broadcast_to(total(acc), (1, 128))
        parts[t, me] = part[t]

        def go(k, carry):
            other = lax.rem(me + k, devs)
            pltpu.make_async_remote_copy(
                src_ref=part.at[t], dst_ref=parts.at[t, me], send_sem=sum_send.at[t],
                recv_sem=sum_recv.at[t],
                device_id=(other // n_grp, lax.rem(other, n_grp)), device_id_type=MESH,
            ).start()
            return carry

        lax.fori_loop(1, devs, go, 0)

    def end_sum(t):
        ref = parts.at[t, everyone]
        pltpu.make_async_copy(ref, ref, sum_recv.at[t]).wait()
        pltpu.make_async_copy(ref, ref, sum_send.at[t]).wait()
        whole = jnp.sum(parts[t], axis=0)
        return whole[0:1, 0:1], whole[1:2, 0:1], whole[2:3, 0:1]

    apply(0, res, wvec)
    start_sum(0, [(res, res), (res, wvec)])
    apply(1, wvec, zvec)
    rr, dq, _ = end_sum(0)
    alpha = rr / dq
    for c in range(4):
        d = res[c]
        q = wvec[c]
        z = zvec[c]
        dvec[c] = d
        qvec[c] = q
        zq[c] = z
        x_out[c] = alpha * d
        res[c] = d - alpha * q
        wvec[c] = q - alpha * z
    start_sum(1, [(res, res), (res, wvec), (res, qvec)])
    apply(2, wvec, zvec)
    new, delta, eps = end_sum(1)
    beta = new / rr
    dq = delta + 2.0 * beta * eps + beta * beta * dq
    rr = new
    alpha = rr / dq
    for c in range(4):
        r = res[c]
        w = wvec[c]
        d = r + beta * dvec[c]
        q = w + beta * qvec[c]
        z = zvec[c] + beta * zq[c]
        dvec[c] = d
        qvec[c] = q
        x_out[c] = x_out[c] + alpha * d
        res[c] = r - alpha * q
        wvec[c] = w - alpha * z
    start_sum(2, [(res, res), (res, wvec), (res, qvec)])
    new, delta, eps = end_sum(2)
    beta = new / rr
    dq = delta + 2.0 * beta * eps + beta * beta * dq
    alpha = new / dq
    for c in range(4):
        r = res[c]
        d = r + beta * dvec[c]
        q = wvec[c] + beta * qvec[c]
        x_out[c] = x_out[c] + alpha * d
        r_out[c] = r - alpha * q


def on_device(samples, block_ids, tile_counts, occupied, coupling):
    n_slab, n_grp = lax.axis_size("slab"), lax.axis_size("grp")
    devs = n_slab * n_grp
    size_x, size_y, size_z = occupied.shape
    slots = samples.shape[0]
    cap = slots // devs
    per = 128 // cap
    span_y = size_y * n_grp
    block_x = block_ids // (span_y * size_z)
    block_y = block_ids // size_z % span_y
    local = (block_x % size_x * size_y + block_y % size_y) * size_z + block_ids % size_z
    me = lax.axis_index("slab") * n_grp + lax.axis_index("grp")
    lanes = jnp.arange(128, dtype=jnp.int32) // cap
    idrows = jnp.tile(local.astype(F32).reshape(devs, cap), (1, per))
    idrows = jnp.where(lanes[None] == me % per, idrows, 0.0).reshape(devs, 1, 128)
    columns = size_x * size_y
    vec = pltpu.VMEM((columns, 64, size_z), F32)
    vmem = pl.BlockSpec(memory_space=pltpu.VMEM)
    shape = jax.ShapeDtypeStruct((columns, 64, size_z), F32)
    x, r = pl.pallas_call(
        functools.partial(kernel, n_slab, n_grp),
        out_shape=(shape, shape),
        in_specs=[vmem] * 5,
        out_specs=(vmem, vmem),
        scratch_shapes=[
            pltpu.VMEM((24, 128, 128), F32),
            pltpu.VMEM((128, 128), F32),
            pltpu.VMEM((devs, cap + 8, 128), F32),
            pltpu.VMEM((devs, cap + 8, 128), F32),
            pltpu.VMEM((576, 192), F32),
            pltpu.VMEM((576, 192), BF16),
            pltpu.VMEM((576, 192), BF16),
            vec,
            pltpu.VMEM((ITERS, 4, 64, size_z), F32),
            pltpu.VMEM((ITERS, 16, 64, size_z), F32),
            vec, vec, vec, vec, vec, vec, vec,
            pltpu.VMEM((ITERS, 8, 128), F32),
            pltpu.VMEM((ITERS, devs, 8, 128), F32),
            pltpu.VMEM((slots, 256), BF16),
            pltpu.SemaphoreType.DMA,
            pltpu.SemaphoreType.DMA,
            pltpu.SemaphoreType.DMA((ITERS, 16)),
            pltpu.SemaphoreType.DMA((ITERS, 16)),
            pltpu.SemaphoreType.DMA((ITERS,)),
            pltpu.SemaphoreType.DMA((ITERS,)),
        ],
        compiler_params=pltpu.CompilerParams(
            collective_id=0, has_side_effects=True, vmem_limit_bytes=40 * 1024 * 1024,
        ),
    )(samples, tile_counts.reshape(slots // 128, 1, 128), idrows,
      occupied.reshape(columns, 1, size_z), coupling)

    def shaped(v):
        return v.transpose(1, 0, 2).reshape(64, size_x, size_y, size_z)

    return shaped(x), shaped(r)


def solution(mesh):
    placed = (
        P(("slab", "grp"), None, None),
        P(("slab", "grp")),
        P(("slab", "grp")),
        P("slab", "grp", None),
        P(),
    )
    return jax.shard_map(
        on_device,
        mesh=mesh,
        in_specs=placed,
        out_specs=(P(None, "slab", "grp", None), P(None, "slab", "grp", None)),
        check_vma=False,
    )
```

```python
import functools

import jax
import jax.numpy as jnp
from jax import lax
from jax.experimental import pallas as pl
from jax.experimental.pallas import tpu as pltpu
from jax.sharding import PartitionSpec as P

ITERS = 3
MESH = pl.DeviceIdType.MESH
F32 = jnp.float32
BF16 = jnp.bfloat16


def hats(u):
    hat, low = [], []
    for j in range(5):
        g = u - float(j)
        h = jnp.maximum(1.0 - jnp.abs(g), 0.0)
        hat.append(h)
        low.append((0.5 + 0.5 * g) * h)
    values = [low[i] + (hat[i + 1] - low[i + 1]) for i in range(4)]
    slopes = [hat[i] - hat[i + 1] for i in range(4)]
    return values, slopes


def split(x):
    hi = x.astype(BF16)
    return hi, (x - hi.astype(F32)).astype(BF16)


def total(x):
    return jnp.sum(jnp.sum(x, axis=0, keepdims=True), axis=1, keepdims=True)


def kernel(n_slab, n_grp, samples, counts, block_ids, occupied, coupling, x_out, r_out,
           held, fac, nodes, send, recv, cs, chi, clo, diag, halo_out, halo_in, image, res, wvec,
           zvec, dvec, qvec, zq, part, parts, weights, held_sem, a2a_send, a2a_recv, halo_send, halo_recv,
           sum_send, sum_recv):
    devs = n_slab * n_grp
    cap = send.shape[1] - 8
    per = 128 // cap
    groups = samples.shape[1] // 128
    size_x, size_y, size_z = occupied.shape
    bits_z = size_z.bit_length() - 1
    bits_y = (size_y * n_grp).bit_length() - 1
    slab = lax.axis_index("slab")
    grp = lax.axis_index("grp")
    me = slab * n_grp + grp

    def group_of(step):
        return lax.rem(me // per + groups // 2 + step, groups)

    def fetch(g):
        rows = pl.ds(pl.multiple_of(g * 128, 128), 128)
        return pltpu.make_async_copy(samples.at[:, rows, :], held.at[g], held_sem.at[g])

    for step in range(groups):
        fetch(group_of(step)).start()
    part[...] = jnp.zeros_like(part)
    barrier = pltpu.get_barrier_semaphore()

    def greet(k, carry):
        other = lax.rem(me + k, devs)
        pl.semaphore_signal(barrier, inc=1, device_id=(other // n_grp, lax.rem(other, n_grp)),
                            device_id_type=MESH)
        return carry

    lax.fori_loop(1, devs, greet, 0)
    pl.semaphore_wait(barrier, devs - 1)

    def splat(step, carry):
        g = group_of(step)
        fetch(g).wait()
        name = block_ids[g]
        z = jnp.bitwise_and(name, size_z - 1)
        y = jnp.bitwise_and(jnp.right_shift(name, bits_z), size_y - 1)
        x = jnp.bitwise_and(jnp.right_shift(name, bits_z + bits_y), size_x - 1)
        name = jnp.broadcast_to(((x * size_y + y) * size_z + z).astype(F32), (8, 128))
        live = lax.broadcasted_iota(jnp.int32, (128, 128), 0) < counts[g]
        for d in range(3):
            values, slopes = hats(4.0 * held[g, d].T)
            normal = 4.0 * held[g, 3 + d].T
            if d == 0:
                normal = jnp.where(live, normal, 0.0)
            for i in range(4):
                fac[8 * d + i] = jnp.where(live, values[i], 0.0) if d == 0 else values[i]
                fac[8 * d + 4 + i] = slopes[i] * normal

        def pair(k, carry):
            j = k // 2
            first = lax.rem(k, 2) * 2

            def add(s, accs):
                at = pl.ds(pl.multiple_of(s * 8, 8), 8)
                v0 = [fac[i, at, :] for i in range(4)]
                s0 = [fac[4 + i, at, :] for i in range(4)]
                v1 = fac[8 + j, at, :]
                s1 = fac[12 + j, at, :]
                out = []
                for e in range(2):
                    v2 = fac[16 + first + e, at, :]
                    s2 = fac[20 + first + e, at, :]
                    p = v1 * v2
                    q = s1 * v2 + v1 * s2
                    for i in range(4):
                        out.append(accs[len(out)] + (s0[i] * p + v0[i] * q))
                    for i in range(4):
                        out.append(accs[len(out)] + v0[i] * p)
                return tuple(out)

            zero = jnp.zeros((8, 128), F32)
            accs = lax.fori_loop(0, 16, add, (zero,) * 16, unroll=True)
            for e in range(2):
                for i in range(8):
                    row = 16 * i + 4 * j + first + e
                    nodes[pl.ds(row, 1), :] = jnp.sum(accs[8 * e + i], axis=0, keepdims=True)
            return carry

        lax.fori_loop(0, 8, pair, 0)
        tiles = nodes[...].T
        for c in range(per):
            target = g * per + c
            send[target, 0:cap, :] = tiles[c * cap:(c + 1) * cap]
            send[target, cap:cap + 8, :] = name

            @pl.when(target != me)
            def _():
                pltpu.make_async_remote_copy(
                    src_ref=send.at[target], dst_ref=recv.at[me],
                    send_sem=a2a_send, recv_sem=a2a_recv,
                    device_id=(target // n_grp, lax.rem(target, n_grp)), device_id_type=MESH,
                ).start()

            @pl.when(target == me)
            def _():
                recv[target] = send[target]
        return carry

    lax.fori_loop(0, groups, splat, 0)

    rowabs = jnp.zeros((64, 64), F32)
    for k in range(27):
        c = 0.5 * (coupling[k] + coupling[26 - k].T)
        rowabs = rowabs + jnp.abs(c)
        base = (2 - k // 9) * 192 + (2 - k // 3 % 3) * 64
        cs[base:base + 64, (k % 3) * 64:(k % 3) * 64 + 64] = c
    hi, lo = split(cs[...])
    chi[...] = hi
    clo[...] = lo
    rowabs = jnp.sum(rowabs, axis=1, keepdims=True) + 0.5
    mask = [occupied[c // 2, c % 2:c % 2 + 1, :].astype(F32) for c in range(4)]
    has = {
        ("x", 0): slab > 0, ("x", 3): slab < n_slab - 1,
        ("y", 0): grp > 0, ("y", 3): grp < n_grp - 1,
    }

    for fx in range(4):
        for fy in range(4):
            sides = [has[k] for k in (("x", fx), ("y", fy)) if k in has]
            if sides:
                @pl.when(jnp.logical_not(functools.reduce(jnp.logical_and, sides)))
                def _():
                    for t in range(ITERS):
                        halo_in[t, fx * 4 + fy] = jnp.zeros((64, 256), F32)

    everyone = pl.ds(0, devs - 1)
    pltpu.make_async_copy(recv.at[everyone], recv.at[everyone], a2a_recv).wait()
    pltpu.make_async_copy(send.at[everyone], send.at[everyone], a2a_send).wait()

    for k in range(groups):
        tiles = recv[k * per:(k + 1) * per, 0:cap, :].reshape(128, 128)
        hi, lo = split(tiles)
        weights[k * 128:(k + 1) * 128, 0:128] = hi
        weights[k * 128:(k + 1) * 128, 128:256] = lo
    bits = cap.bit_length() - 1
    lanes = jnp.right_shift(lax.broadcasted_iota(jnp.int32, (devs, 128), 1), bits)
    source = jnp.bitwise_and(lax.broadcasted_iota(jnp.int32, (devs, 128), 0), per - 1)
    names = jnp.where(lanes == lax.rem(me, per), recv[:, cap, :], 0.0)
    shift = cap
    while shift < 128:
        names = names + pltpu.roll(names, shift, 1)
        shift *= 2
    names = jnp.where(lanes == source, names, 0.0)
    ids = [jnp.sum(names[k * per:(k + 1) * per], axis=0, keepdims=True) for k in range(groups)]
    ids = jnp.concatenate(ids, axis=1).astype(jnp.int32)
    lane = lax.broadcasted_iota(jnp.int32, (64, 256), 1)

    def frame(fx, fy, m):
        up = jnp.where(lane == 0, 0.0, pltpu.roll(m, 1, 1))
        down = jnp.where(lane == 255, 0.0, pltpu.roll(m, 255, 1))
        hi, lo = split(jnp.concatenate([up, m, down], axis=0))
        xs = [x for x in range(2) if 0 <= fx - x <= 2]
        ys = [y for y in range(2) if 0 <= fy - y <= 2]
        size = 64 * len(ys)
        starts = [(2 - (fx - x)) * 192 + (2 - (fy - ys[0])) * 64 for x in xs]
        high = [chi[s:s + size, :] for s in starts]
        low = [clo[s:s + size, :] for s in starts]
        rows = size * len(xs)
        first = jnp.dot(jnp.concatenate(high + low, axis=0), hi, preferred_element_type=F32)
        second = jnp.dot(jnp.concatenate(high, axis=0), lo, preferred_element_type=F32)
        sums = first[0:rows] + (first[rows:2 * rows] + second)
        for a, x in enumerate(xs):
            for b, y in enumerate(ys):
                at = a * size + b * 64
                image[2 * x + y] += sums[at:at + 64]

    def both(a, b):
        return jnp.logical_and(a, b)

    def send_copy(t, src, f, dev):
        return pltpu.make_async_remote_copy(
            src_ref=src, dst_ref=halo_in.at[t, f], send_sem=halo_send.at[t, f],
            recv_sem=halo_recv.at[t, f], device_id=dev, device_id_type=MESH)

    def column_sends(t, c):
        x, y = c // 2, c % 2
        ref = halo_out.at[t, c]
        along_x = (slab + 1, grp) if x == 1 else (slab - 1, grp)
        along_y = (slab, grp + 1) if y == 1 else (slab, grp - 1)
        fx, fy = (0, 3)[x == 0], (0, 3)[y == 0]
        return [(has["x", 3 - fx], ref, fx * 4 + 1 + y, along_x),
                (has["y", 3 - fy], ref, (1 + x) * 4 + fy, along_y)]

    def corner_send(t, fx, y):
        f = fx * 4 + 1 + y
        corner = fx * 4 + (0 if y == 1 else 3)
        dev = (slab, grp + 1) if y == 1 else (slab, grp - 1)
        cond = both(has["x", fx], has["y", 3 if y == 1 else 0])
        return cond, halo_in.at[t, f], corner, dev

    def start(t, cond, ref, f, dev):
        @pl.when(cond)
        def _():
            send_copy(t, ref, f, dev).start()

    def arrived(t, cond, f):
        @pl.when(cond)
        def _():
            send_copy(t, halo_in.at[t, f], f, (slab, grp)).wait_recv()

    def offer(t, c, value):
        halo_out[t, c] = mask[c] * value
        for send_one in column_sends(t, c):
            start(t, *send_one)

    def apply(t, src, dst):
        for c in range(4):
            image[c] = jnp.zeros((64, 256), F32)
        for c in range(4):
            frame(1 + c // 2, 1 + c % 2, halo_out[t, c])
        for y in (0, 1):
            for fx in (0, 3):
                arrived(t, has["x", fx], fx * 4 + 1 + y)
                start(t, *corner_send(t, fx, y))
            for x in (0, 1):
                arrived(t, has["y", 3 * y], (1 + x) * 4 + 3 * y)
            for x in (0, 1):
                frame(1 + x, 3 * y, halo_in[t, (1 + x) * 4 + 3 * y])
        for fx in (0, 3):
            for y in (0, 1):
                frame(fx, 1 + y, halo_in[t, fx * 4 + 1 + y])
        for fx in (0, 3):
            for fy in (0, 3):
                arrived(t, both(has["x", fx], has["y", fy]), fx * 4 + fy)
        for fx in (0, 3):
            for fy in (0, 3):
                frame(fx, fy, halo_in[t, fx * 4 + fy])
        for c in range(4):
            dst[c] = diag[c] * src[c] - mask[c] * image[c]
        for c in range(4):
            for cond, ref, f, dev in column_sends(t, c):
                @pl.when(cond)
                def _():
                    send_copy(t, ref, f, dev).wait_send()
        for fx in (0, 3):
            for y in (0, 1):
                cond, ref, f, dev = corner_send(t, fx, y)

                @pl.when(cond)
                def _():
                    send_copy(t, ref, f, dev).wait_send()

    def start_sum(t, pairs):
        for k, (a, b) in enumerate(pairs):
            acc = a[0] * b[0]
            for c in range(1, 4):
                acc = acc + a[c] * b[c]
            part[t, k:k + 1, :] = jnp.broadcast_to(total(acc), (1, 128))
        parts[t, me] = part[t]

        def go(k, carry):
            other = lax.rem(me + k, devs)
            pltpu.make_async_remote_copy(
                src_ref=part.at[t], dst_ref=parts.at[t, me], send_sem=sum_send.at[t],
                recv_sem=sum_recv.at[t],
                device_id=(other // n_grp, lax.rem(other, n_grp)), device_id_type=MESH,
            ).start()
            return carry

        lax.fori_loop(1, devs, go, 0)

    def end_sum(t):
        ref = parts.at[t, everyone]
        pltpu.make_async_copy(ref, ref, sum_recv.at[t]).wait()
        pltpu.make_async_copy(ref, ref, sum_send.at[t]).wait()
        whole = jnp.sum(parts[t], axis=0)
        return whole[0:1, 0:1], whole[1:2, 0:1], whole[2:3, 0:1]

    for c in range(4):
        place = lax.broadcasted_iota(jnp.int32, (256, 1024), 0) + 256 * c
        hot = jnp.where(place == ids, 1.0, 0.0).astype(BF16)
        block = jnp.dot(hot, weights[...], preferred_element_type=F32)
        block = (block[:, 0:128] + block[:, 128:256]).T
        res[c] = block[0:64]
        offer(0, c, block[0:64])
        diag[c] = rowabs + 4.0 * block[64:128]

    apply(0, res, wvec)
    for c in range(4):
        offer(1, c, wvec[c])
    start_sum(0, [(res, res), (res, wvec)])
    apply(1, wvec, zvec)
    rr, dq, _ = end_sum(0)
    alpha = rr / dq
    for c in range(4):
        d = res[c]
        q = wvec[c]
        z = zvec[c]
        dvec[c] = d
        qvec[c] = q
        zq[c] = z
        x_out[c] = alpha * d
        res[c] = d - alpha * q
        w = q - alpha * z
        wvec[c] = w
        offer(2, c, w)
    start_sum(1, [(res, res), (res, wvec), (res, qvec)])
    apply(2, wvec, zvec)
    new, delta, eps = end_sum(1)
    beta = new / rr
    dq = delta + 2.0 * beta * eps + beta * beta * dq
    rr = new
    alpha = rr / dq
    for c in range(4):
        r = res[c]
        w = wvec[c]
        d = r + beta * dvec[c]
        q = w + beta * qvec[c]
        z = zvec[c] + beta * zq[c]
        dvec[c] = d
        qvec[c] = q
        x_out[c] = x_out[c] + alpha * d
        res[c] = r - alpha * q
        wvec[c] = w - alpha * z
    start_sum(2, [(res, res), (res, wvec), (res, qvec)])
    new, delta, eps = end_sum(2)
    beta = new / rr
    dq = delta + 2.0 * beta * eps + beta * beta * dq
    alpha = new / dq
    for c in range(4):
        r = res[c]
        d = r + beta * dvec[c]
        q = wvec[c] + beta * qvec[c]
        x_out[c] = x_out[c] + alpha * d
        r_out[c] = r - alpha * q


def on_device(samples, block_ids, tile_counts, occupied, coupling):
    n_slab, n_grp = lax.axis_size("slab"), lax.axis_size("grp")
    devs = n_slab * n_grp
    size_x, size_y, size_z = occupied.shape
    slots = samples.shape[0]
    cap = slots // devs
    columns = size_x * size_y
    vec = pltpu.VMEM((columns, 64, size_z), F32)
    vmem = pl.BlockSpec(memory_space=pltpu.VMEM)
    shape = jax.ShapeDtypeStruct((columns, 64, size_z), F32)
    x, r = pl.pallas_call(
        functools.partial(kernel, n_slab, n_grp),
        out_shape=(shape, shape),
        in_specs=[pl.BlockSpec(memory_space=pl.ANY)] + [vmem] * 4,
        out_specs=(vmem, vmem),
        scratch_shapes=[
            pltpu.VMEM((slots // 128, 6, 128, 128), F32),
            pltpu.VMEM((24, 128, 128), F32),
            pltpu.VMEM((128, 128), F32),
            pltpu.VMEM((devs, cap + 8, 128), F32),
            pltpu.VMEM((devs, cap + 8, 128), F32),
            pltpu.VMEM((576, 192), F32),
            pltpu.VMEM((576, 192), BF16),
            pltpu.VMEM((576, 192), BF16),
            vec,
            pltpu.VMEM((ITERS, 4, 64, size_z), F32),
            pltpu.VMEM((ITERS, 16, 64, size_z), F32),
            vec, vec, vec, vec, vec, vec, vec,
            pltpu.VMEM((ITERS, 8, 128), F32),
            pltpu.VMEM((ITERS, devs, 8, 128), F32),
            pltpu.VMEM((slots, 256), BF16),
            pltpu.SemaphoreType.DMA((slots // 128,)),
            pltpu.SemaphoreType.DMA,
            pltpu.SemaphoreType.DMA,
            pltpu.SemaphoreType.DMA((ITERS, 16)),
            pltpu.SemaphoreType.DMA((ITERS, 16)),
            pltpu.SemaphoreType.DMA((ITERS,)),
            pltpu.SemaphoreType.DMA((ITERS,)),
        ],
        compiler_params=pltpu.CompilerParams(
            collective_id=0, has_side_effects=True, vmem_limit_bytes=40 * 1024 * 1024,
        ),
    )(samples.transpose(1, 0, 2), tile_counts.reshape(slots // 128, 1, 128),
      block_ids.reshape(slots // 128, 1, 128), occupied, coupling)

    def shaped(v):
        return v.transpose(1, 0, 2).reshape(64, size_x, size_y, size_z)

    return shaped(x), shaped(r)


def solution(mesh):
    placed = (
        P(("slab", "grp"), None, None),
        P(("slab", "grp")),
        P(("slab", "grp")),
        P("slab", "grp", None),
        P(),
    )
    return jax.shard_map(
        on_device,
        mesh=mesh,
        in_specs=placed,
        out_specs=(P(None, "slab", "grp", None), P(None, "slab", "grp", None)),
        check_vma=False,
    )
```

```python
import functools

import jax
import jax.numpy as jnp
from jax import lax
from jax.experimental import pallas as pl
from jax.experimental.pallas import tpu as pltpu
from jax.sharding import PartitionSpec as P

ITERS = 3
MESH = pl.DeviceIdType.MESH
F32 = jnp.float32
BF16 = jnp.bfloat16


def hats(u):
    hat, low = [], []
    for j in range(5):
        g = u - float(j)
        h = jnp.maximum(1.0 - jnp.abs(g), 0.0)
        hat.append(h)
        low.append((0.5 + 0.5 * g) * h)
    values = [low[i] + (hat[i + 1] - low[i + 1]) for i in range(4)]
    slopes = [hat[i] - hat[i + 1] for i in range(4)]
    return values, slopes


def fold(rows):
    place = lax.broadcasted_iota(jnp.int32, (8, 128), 0)
    step = 1
    while len(rows) > 1:
        keep = jnp.bitwise_and(place, step) == 0
        rows = [
            jnp.where(keep, a, b) + pltpu.roll(jnp.where(keep, b, a), 8 - step, 0)
            for a, b in zip(rows[0::2], rows[1::2])
        ]
        step *= 2
    return rows[0]


def split(x):
    hi = x.astype(BF16)
    return hi, (x - hi.astype(F32)).astype(BF16)


def total(x):
    return jnp.sum(jnp.sum(x, axis=0, keepdims=True), axis=1, keepdims=True)


def kernel(n_slab, n_grp, samples, *refs):
    (count_in, name_in, occupied_in, coupling_in, x_out, r_out, counts, block_ids, occupied,
     coupling, held, fac, nodes, send, recv, cs, chi, clo, diag, halo_out, halo_in, image, res, wvec,
     zvec, dvec, qvec, zq, part, parts, weights, held_sem, a2a_send, a2a_recv, halo_send, halo_recv,
     sum_send, sum_recv, in_sem) = refs
    devs = n_slab * n_grp
    cap = send.shape[1] - 8
    per = 128 // cap
    groups = samples.shape[1] // 128
    size_x, size_y, size_z = occupied.shape
    bits_z = size_z.bit_length() - 1
    bits_y = (size_y * n_grp).bit_length() - 1
    slab = lax.axis_index("slab")
    grp = lax.axis_index("grp")
    me = slab * n_grp + grp

    def group_of(step):
        return lax.rem(me // per + groups // 2 + step, groups)

    def fetch(g):
        rows = pl.ds(pl.multiple_of(g * 128, 128), 128)
        return pltpu.make_async_copy(samples.at[:, rows, :], held.at[g], held_sem.at[g])

    small = [(count_in, counts), (name_in, block_ids), (occupied_in, occupied),
             (coupling_in, coupling)]
    small = [pltpu.make_async_copy(a, b, in_sem.at[k]) for k, (a, b) in enumerate(small)]
    small[0].start()
    small[1].start()
    for step in range(groups):
        fetch(group_of(step)).start()
    small[2].start()
    small[3].start()
    part[...] = jnp.zeros_like(part)
    barrier = pltpu.get_barrier_semaphore()

    def greet(k, carry):
        other = lax.rem(me + k, devs)
        pl.semaphore_signal(barrier, inc=1, device_id=(other // n_grp, lax.rem(other, n_grp)),
                            device_id_type=MESH)
        return carry

    lax.fori_loop(1, devs, greet, 0)
    pl.semaphore_wait(barrier, devs - 1)

    small[0].wait()
    small[1].wait()

    def splat(step, carry):
        g = group_of(step)
        fetch(g).wait()
        name = block_ids[g]
        z = jnp.bitwise_and(name, size_z - 1)
        y = jnp.bitwise_and(jnp.right_shift(name, bits_z), size_y - 1)
        x = jnp.bitwise_and(jnp.right_shift(name, bits_z + bits_y), size_x - 1)
        name = jnp.broadcast_to(((x * size_y + y) * size_z + z).astype(F32), (8, 128))
        live = lax.broadcasted_iota(jnp.int32, (128, 128), 0) < counts[g]
        for d in range(3):
            values, slopes = hats(4.0 * held[g, d].T)
            normal = 4.0 * held[g, 3 + d].T
            if d == 0:
                normal = jnp.where(live, normal, 0.0)
            for i in range(4):
                fac[8 * d + i] = jnp.where(live, values[i], 0.0) if d == 0 else values[i]
                fac[8 * d + 4 + i] = slopes[i] * normal

        def pair(k, carry):
            i = k // 2
            first = lax.rem(k, 2) * 2

            def add(s, accs):
                at = pl.ds(pl.multiple_of(s * 8, 8), 8)
                v0 = fac[i, at, :]
                s0 = fac[4 + i, at, :]
                v2 = [fac[16 + l, at, :] for l in range(4)]
                s2 = [fac[20 + l, at, :] for l in range(4)]
                rhs, dens = [], []
                for e in range(2):
                    v1 = fac[8 + first + e, at, :]
                    s1 = fac[12 + first + e, at, :]
                    p = v0 * v1
                    q = s0 * v1 + v0 * s1
                    for l in range(4):
                        rhs.append(accs[4 * e + l] + (v2[l] * q + s2[l] * p))
                        dens.append(accs[8 + 4 * e + l] + v2[l] * p)
                return tuple(rhs + dens)

            zero = jnp.zeros((8, 128), F32)
            accs = lax.fori_loop(0, 16, add, (zero,) * 16, unroll=True)
            base = pl.multiple_of(8 * k, 8)
            nodes[pl.ds(base, 8), :] = fold(accs[0:8])
            nodes[pl.ds(64 + base, 8), :] = fold(accs[8:16])
            return carry

        lax.fori_loop(0, 8, pair, 0)
        tiles = nodes[...].T
        for c in range(per):
            target = g * per + c
            send[target, 0:cap, :] = tiles[c * cap:(c + 1) * cap]
            send[target, cap:cap + 8, :] = name

            @pl.when(target != me)
            def _():
                pltpu.make_async_remote_copy(
                    src_ref=send.at[target], dst_ref=recv.at[me],
                    send_sem=a2a_send, recv_sem=a2a_recv,
                    device_id=(target // n_grp, lax.rem(target, n_grp)), device_id_type=MESH,
                ).start()

            @pl.when(target == me)
            def _():
                recv[target] = send[target]
        return carry

    lax.fori_loop(0, groups, splat, 0)

    small[2].wait()
    small[3].wait()

    rowabs = jnp.zeros((64, 64), F32)
    for k in range(27):
        c = 0.5 * (coupling[k] + coupling[26 - k].T)
        rowabs = rowabs + jnp.abs(c)
        base = (2 - k // 9) * 192 + (2 - k // 3 % 3) * 64
        cs[base:base + 64, (k % 3) * 64:(k % 3) * 64 + 64] = c
    hi, lo = split(cs[...])
    chi[...] = hi
    clo[...] = lo
    rowabs = jnp.sum(rowabs, axis=1, keepdims=True) + 0.5
    mask = [occupied[c // 2, c % 2:c % 2 + 1, :].astype(F32) for c in range(4)]
    has = {
        ("x", 0): slab > 0, ("x", 3): slab < n_slab - 1,
        ("y", 0): grp > 0, ("y", 3): grp < n_grp - 1,
    }

    for fx in range(4):
        for fy in range(4):
            sides = [has[k] for k in (("x", fx), ("y", fy)) if k in has]
            if sides:
                @pl.when(jnp.logical_not(functools.reduce(jnp.logical_and, sides)))
                def _():
                    for t in range(ITERS):
                        halo_in[t, fx * 4 + fy] = jnp.zeros((64, 256), F32)

    everyone = pl.ds(0, devs - 1)
    pltpu.make_async_copy(recv.at[everyone], recv.at[everyone], a2a_recv).wait()
    pltpu.make_async_copy(send.at[everyone], send.at[everyone], a2a_send).wait()

    for k in range(groups):
        tiles = recv[k * per:(k + 1) * per, 0:cap, :].reshape(128, 128)
        hi, lo = split(tiles)
        weights[k * 128:(k + 1) * 128, 0:128] = hi
        weights[k * 128:(k + 1) * 128, 128:256] = lo
    bits = cap.bit_length() - 1
    lanes = jnp.right_shift(lax.broadcasted_iota(jnp.int32, (devs, 128), 1), bits)
    source = jnp.bitwise_and(lax.broadcasted_iota(jnp.int32, (devs, 128), 0), per - 1)
    names = jnp.where(lanes == lax.rem(me, per), recv[:, cap, :], 0.0)
    shift = cap
    while shift < 128:
        names = names + pltpu.roll(names, shift, 1)
        shift *= 2
    names = jnp.where(lanes == source, names, 0.0)
    ids = [jnp.sum(names[k * per:(k + 1) * per], axis=0, keepdims=True) for k in range(groups)]
    ids = jnp.concatenate(ids, axis=1).astype(jnp.int32)
    lane = lax.broadcasted_iota(jnp.int32, (64, 256), 1)

    def frame(fx, fy, m):
        up = jnp.where(lane == 0, 0.0, pltpu.roll(m, 1, 1))
        down = jnp.where(lane == 255, 0.0, pltpu.roll(m, 255, 1))
        hi, lo = split(jnp.concatenate([up, m, down], axis=0))
        xs = [x for x in range(2) if 0 <= fx - x <= 2]
        ys = [y for y in range(2) if 0 <= fy - y <= 2]
        size = 64 * len(ys)
        starts = [(2 - (fx - x)) * 192 + (2 - (fy - ys[0])) * 64 for x in xs]
        high = [chi[s:s + size, :] for s in starts]
        low = [clo[s:s + size, :] for s in starts]
        rows = size * len(xs)
        first = jnp.dot(jnp.concatenate(high + low, axis=0), hi, preferred_element_type=F32)
        second = jnp.dot(jnp.concatenate(high, axis=0), lo, preferred_element_type=F32)
        sums = first[0:rows] + (first[rows:2 * rows] + second)
        for a, x in enumerate(xs):
            for b, y in enumerate(ys):
                at = a * size + b * 64
                image[2 * x + y] += sums[at:at + 64]

    def both(a, b):
        return jnp.logical_and(a, b)

    def send_copy(t, src, f, dev):
        return pltpu.make_async_remote_copy(
            src_ref=src, dst_ref=halo_in.at[t, f], send_sem=halo_send.at[t, f],
            recv_sem=halo_recv.at[t, f], device_id=dev, device_id_type=MESH)

    def column_sends(t, c):
        x, y = c // 2, c % 2
        ref = halo_out.at[t, c]
        along_x = (slab + 1, grp) if x == 1 else (slab - 1, grp)
        along_y = (slab, grp + 1) if y == 1 else (slab, grp - 1)
        fx, fy = (0, 3)[x == 0], (0, 3)[y == 0]
        return [(has["x", 3 - fx], ref, fx * 4 + 1 + y, along_x),
                (has["y", 3 - fy], ref, (1 + x) * 4 + fy, along_y)]

    def corner_send(t, fx, y):
        f = fx * 4 + 1 + y
        corner = fx * 4 + (0 if y == 1 else 3)
        dev = (slab, grp + 1) if y == 1 else (slab, grp - 1)
        cond = both(has["x", fx], has["y", 3 if y == 1 else 0])
        return cond, halo_in.at[t, f], corner, dev

    def start(t, cond, ref, f, dev):
        @pl.when(cond)
        def _():
            send_copy(t, ref, f, dev).start()

    def arrived(t, cond, f):
        @pl.when(cond)
        def _():
            send_copy(t, halo_in.at[t, f], f, (slab, grp)).wait_recv()

    def offer(t, c, value):
        halo_out[t, c] = mask[c] * value
        for send_one in column_sends(t, c):
            start(t, *send_one)

    def apply(t, src, dst):
        for c in range(4):
            image[c] = jnp.zeros((64, 256), F32)
        for c in range(4):
            frame(1 + c // 2, 1 + c % 2, halo_out[t, c])
        for y in (0, 1):
            for fx in (0, 3):
                arrived(t, has["x", fx], fx * 4 + 1 + y)
                start(t, *corner_send(t, fx, y))
            for x in (0, 1):
                arrived(t, has["y", 3 * y], (1 + x) * 4 + 3 * y)
            for x in (0, 1):
                frame(1 + x, 3 * y, halo_in[t, (1 + x) * 4 + 3 * y])
        for fx in (0, 3):
            for y in (0, 1):
                frame(fx, 1 + y, halo_in[t, fx * 4 + 1 + y])
        for fx in (0, 3):
            for fy in (0, 3):
                arrived(t, both(has["x", fx], has["y", fy]), fx * 4 + fy)
        for fx in (0, 3):
            for fy in (0, 3):
                frame(fx, fy, halo_in[t, fx * 4 + fy])
        for c in range(4):
            dst[c] = diag[c] * src[c] - mask[c] * image[c]
        for c in range(4):
            for cond, ref, f, dev in column_sends(t, c):
                @pl.when(cond)
                def _():
                    send_copy(t, ref, f, dev).wait_send()
        for fx in (0, 3):
            for y in (0, 1):
                cond, ref, f, dev = corner_send(t, fx, y)

                @pl.when(cond)
                def _():
                    send_copy(t, ref, f, dev).wait_send()

    def start_sum(t, pairs):
        for k, (a, b) in enumerate(pairs):
            acc = a[0] * b[0]
            for c in range(1, 4):
                acc = acc + a[c] * b[c]
            part[t, k:k + 1, :] = jnp.broadcast_to(total(acc), (1, 128))
        parts[t, me] = part[t]

        def go(k, carry):
            other = lax.rem(me + k, devs)
            pltpu.make_async_remote_copy(
                src_ref=part.at[t], dst_ref=parts.at[t, me], send_sem=sum_send.at[t],
                recv_sem=sum_recv.at[t],
                device_id=(other // n_grp, lax.rem(other, n_grp)), device_id_type=MESH,
            ).start()
            return carry

        lax.fori_loop(1, devs, go, 0)

    def end_sum(t):
        ref = parts.at[t, everyone]
        pltpu.make_async_copy(ref, ref, sum_recv.at[t]).wait()
        pltpu.make_async_copy(ref, ref, sum_send.at[t]).wait()
        whole = jnp.sum(parts[t], axis=0)
        return whole[0:1, 0:1], whole[1:2, 0:1], whole[2:3, 0:1]

    for c in range(4):
        place = lax.broadcasted_iota(jnp.int32, (256, 1024), 0) + 256 * c
        hot = jnp.where(place == ids, 1.0, 0.0).astype(BF16)
        block = jnp.dot(hot, weights[...], preferred_element_type=F32)
        block = (block[:, 0:128] + block[:, 128:256]).T
        res[c] = block[0:64]
        offer(0, c, block[0:64])
        diag[c] = rowabs + 4.0 * block[64:128]

    apply(0, res, wvec)
    for c in range(4):
        offer(1, c, wvec[c])
    start_sum(0, [(res, res), (res, wvec)])
    apply(1, wvec, zvec)
    rr, dq, _ = end_sum(0)
    alpha = rr / dq
    for c in range(4):
        d = res[c]
        q = wvec[c]
        z = zvec[c]
        dvec[c] = d
        qvec[c] = q
        zq[c] = z
        x_out[c] = alpha * d
        res[c] = d - alpha * q
        w = q - alpha * z
        wvec[c] = w
        offer(2, c, w)
    start_sum(1, [(res, res), (res, wvec), (res, qvec)])
    apply(2, wvec, zvec)
    new, delta, eps = end_sum(1)
    beta = new / rr
    dq = delta + 2.0 * beta * eps + beta * beta * dq
    rr = new
    alpha = rr / dq
    for c in range(4):
        r = res[c]
        w = wvec[c]
        d = r + beta * dvec[c]
        q = w + beta * qvec[c]
        z = zvec[c] + beta * zq[c]
        dvec[c] = d
        qvec[c] = q
        x_out[c] = x_out[c] + alpha * d
        res[c] = r - alpha * q
        wvec[c] = w - alpha * z
    start_sum(2, [(res, res), (res, wvec), (res, qvec)])
    new, delta, eps = end_sum(2)
    beta = new / rr
    dq = delta + 2.0 * beta * eps + beta * beta * dq
    alpha = new / dq
    for c in range(4):
        r = res[c]
        d = r + beta * dvec[c]
        q = wvec[c] + beta * qvec[c]
        x_out[c] = x_out[c] + alpha * d
        r_out[c] = r - alpha * q


def on_device(samples, block_ids, tile_counts, occupied, coupling):
    n_slab, n_grp = lax.axis_size("slab"), lax.axis_size("grp")
    devs = n_slab * n_grp
    size_x, size_y, size_z = occupied.shape
    slots = samples.shape[0]
    cap = slots // devs
    columns = size_x * size_y
    vec = pltpu.VMEM((columns, 64, size_z), F32)
    vmem = pl.BlockSpec(memory_space=pltpu.VMEM)
    shape = jax.ShapeDtypeStruct((columns, 64, size_z), F32)
    x, r = pl.pallas_call(
        functools.partial(kernel, n_slab, n_grp),
        out_shape=(shape, shape),
        in_specs=[pl.BlockSpec(memory_space=pl.ANY)] * 5,
        out_specs=(vmem, vmem),
        scratch_shapes=[
            pltpu.VMEM((slots // 128, 1, 128), jnp.int32),
            pltpu.VMEM((slots // 128, 1, 128), jnp.int32),
            pltpu.VMEM(occupied.shape, jnp.int32),
            pltpu.VMEM(coupling.shape, F32),
            pltpu.VMEM((slots // 128, 6, 128, 128), F32),
            pltpu.VMEM((24, 128, 128), F32),
            pltpu.VMEM((128, 128), F32),
            pltpu.VMEM((devs, cap + 8, 128), F32),
            pltpu.VMEM((devs, cap + 8, 128), F32),
            pltpu.VMEM((576, 192), F32),
            pltpu.VMEM((576, 192), BF16),
            pltpu.VMEM((576, 192), BF16),
            vec,
            pltpu.VMEM((ITERS, 4, 64, size_z), F32),
            pltpu.VMEM((ITERS, 16, 64, size_z), F32),
            vec, vec, vec, vec, vec, vec, vec,
            pltpu.VMEM((ITERS, 8, 128), F32),
            pltpu.VMEM((ITERS, devs, 8, 128), F32),
            pltpu.VMEM((slots, 256), BF16),
            pltpu.SemaphoreType.DMA((slots // 128,)),
            pltpu.SemaphoreType.DMA,
            pltpu.SemaphoreType.DMA,
            pltpu.SemaphoreType.DMA((ITERS, 16)),
            pltpu.SemaphoreType.DMA((ITERS, 16)),
            pltpu.SemaphoreType.DMA((ITERS,)),
            pltpu.SemaphoreType.DMA((ITERS,)),
            pltpu.SemaphoreType.DMA((4,)),
        ],
        compiler_params=pltpu.CompilerParams(
            collective_id=0, has_side_effects=True, vmem_limit_bytes=60 * 1024 * 1024,
        ),
    )(samples.transpose(1, 0, 2), tile_counts.reshape(slots // 128, 1, 128),
      block_ids.reshape(slots // 128, 1, 128), occupied, coupling)

    def shaped(v):
        return v.transpose(1, 0, 2).reshape(64, size_x, size_y, size_z)

    return shaped(x), shaped(r)


def solution(mesh):
    placed = (
        P(("slab", "grp"), None, None),
        P(("slab", "grp")),
        P(("slab", "grp")),
        P("slab", "grp", None),
        P(),
    )
    return jax.shard_map(
        on_device,
        mesh=mesh,
        in_specs=placed,
        out_specs=(P(None, "slab", "grp", None), P(None, "slab", "grp", None)),
        check_vma=False,
    )
```

```python
import functools

import jax
import jax.numpy as jnp
from jax import lax
from jax.experimental import pallas as pl
from jax.experimental.pallas import tpu as pltpu
from jax.sharding import PartitionSpec as P

ITERS = 3
MESH = pl.DeviceIdType.MESH
F32 = jnp.float32
BF16 = jnp.bfloat16


def hats(u):
    hat, low = [], []
    for j in range(5):
        g = u - float(j)
        h = jnp.maximum(1.0 - jnp.abs(g), 0.0)
        hat.append(h)
        low.append((0.5 + 0.5 * g) * h)
    values = [low[i] + (hat[i + 1] - low[i + 1]) for i in range(4)]
    slopes = [hat[i] - hat[i + 1] for i in range(4)]
    return values, slopes


def fold(rows):
    place = lax.broadcasted_iota(jnp.int32, (8, 128), 0)
    step = 1
    while len(rows) > 1:
        keep = jnp.bitwise_and(place, step) == 0
        rows = [
            jnp.where(keep, a, b) + pltpu.roll(jnp.where(keep, b, a), 8 - step, 0)
            for a, b in zip(rows[0::2], rows[1::2])
        ]
        step *= 2
    return rows[0]


def split(x):
    hi = x.astype(BF16)
    return hi, (x - hi.astype(F32)).astype(BF16)


def total(x):
    return jnp.sum(jnp.sum(x, axis=0, keepdims=True), axis=1, keepdims=True)


def kernel(n_slab, n_grp, samples, *refs):
    (count_in, name_in, occupied_in, coupling_in, x_out, r_out, counts, block_ids, occupied,
     coupling, held, fac, nodes, send, recv, cs, deep, diag, halo_out, halo_in, image, res, wvec,
     zvec, dvec, qvec, zq, part, parts, weights, held_sem, a2a_send, a2a_recv, halo_send, halo_recv,
     sum_send, sum_recv, in_sem) = refs
    devs = n_slab * n_grp
    cap = send.shape[1] - 1
    per = 128 // cap
    groups = samples.shape[1] // 128
    share = groups // n_slab
    size_x, size_y, size_z = occupied.shape
    bits_z = size_z.bit_length() - 1
    bits_y = (size_y * n_grp).bit_length() - 1
    slab = lax.axis_index("slab")
    grp = lax.axis_index("grp")
    me = slab * n_grp + grp

    def group_of(step):
        k = step // share
        away = jnp.where(k < n_slab // 2, k + n_slab // 2, n_slab - 1 - k)
        return lax.rem(slab + away, n_slab) * share + lax.rem(step, share)

    def fetch(g):
        rows = pl.ds(pl.multiple_of(g * 128, 128), 128)
        return pltpu.make_async_copy(samples.at[:, rows, :], held.at[g], held_sem.at[g])

    small = [(count_in, counts), (name_in, block_ids), (occupied_in, occupied),
             (coupling_in, coupling)]
    small = [pltpu.make_async_copy(a, b, in_sem.at[k]) for k, (a, b) in enumerate(small)]
    small[0].start()
    small[1].start()
    for step in range(groups):
        fetch(group_of(step)).start()
    small[2].start()
    small[3].start()
    part[...] = jnp.zeros_like(part)
    barrier = pltpu.get_barrier_semaphore()

    def greet(k, carry):
        other = lax.rem(me + k, devs)
        pl.semaphore_signal(barrier, inc=1, device_id=(other // n_grp, lax.rem(other, n_grp)),
                            device_id_type=MESH)
        return carry

    lax.fori_loop(1, devs, greet, 0)

    small[0].wait()
    small[1].wait()

    def splat(step, carry):
        g = group_of(step)
        fetch(g).wait()
        name = block_ids[g]
        z = jnp.bitwise_and(name, size_z - 1)
        y = jnp.bitwise_and(jnp.right_shift(name, bits_z), size_y - 1)
        x = jnp.bitwise_and(jnp.right_shift(name, bits_z + bits_y), size_x - 1)
        name = ((x * size_y + y) * size_z + z).astype(F32)
        live = lax.broadcasted_iota(jnp.int32, (128, 128), 0) < counts[g]
        for d in range(3):
            values, slopes = hats(4.0 * held[g, d].T)
            normal = 4.0 * held[g, 3 + d].T
            if d == 0:
                normal = jnp.where(live, normal, 0.0)
            for i in range(4):
                fac[8 * d + i] = jnp.where(live, values[i], 0.0) if d == 0 else values[i]
                fac[8 * d + 4 + i] = slopes[i] * normal

        def pair(k, carry):
            i = k // 2
            first = lax.rem(k, 2) * 2

            def add(s, accs):
                at = pl.ds(pl.multiple_of(s * 8, 8), 8)
                v0 = fac[i, at, :]
                s0 = fac[4 + i, at, :]
                v2 = [fac[16 + l, at, :] for l in range(4)]
                s2 = [fac[20 + l, at, :] for l in range(4)]
                rhs, dens = [], []
                for e in range(2):
                    v1 = fac[8 + first + e, at, :]
                    s1 = fac[12 + first + e, at, :]
                    p = v0 * v1
                    q = s0 * v1 + v0 * s1
                    for l in range(4):
                        rhs.append(accs[4 * e + l] + (v2[l] * q + s2[l] * p))
                        dens.append(accs[8 + 4 * e + l] + v2[l] * p)
                return tuple(rhs + dens)

            zero = jnp.zeros((8, 128), F32)
            accs = lax.fori_loop(0, 16, add, (zero,) * 16, unroll=True)
            base = pl.multiple_of(8 * k, 8)
            nodes[pl.ds(base, 8), :] = fold(accs[0:8])
            nodes[pl.ds(64 + base, 8), :] = fold(accs[8:16])
            return carry

        lax.fori_loop(0, 8, pair, 0)
        tiles = nodes[...].T

        @pl.when(step == 0)
        def _():
            pl.semaphore_wait(barrier, devs - 1)

        for c in range(per):
            target = g * per + c
            send[target, 0:cap, :] = tiles[c * cap:(c + 1) * cap]
            send[target, cap:cap + 1, :] = name

            @pl.when(target != me)
            def _():
                pltpu.make_async_remote_copy(
                    src_ref=send.at[target], dst_ref=recv.at[me],
                    send_sem=a2a_send, recv_sem=a2a_recv,
                    device_id=(target // n_grp, lax.rem(target, n_grp)), device_id_type=MESH,
                ).start()

            @pl.when(target == me)
            def _():
                recv[target] = send[target]
        return carry

    lax.fori_loop(0, groups, splat, 0)

    small[2].wait()
    small[3].wait()

    rowabs = jnp.zeros((64, 64), F32)
    for k in range(27):
        c = 0.5 * (coupling[k] + coupling[26 - k].T)
        rowabs = rowabs + jnp.abs(c)
        base = (2 - k // 9) * 192 + (2 - k // 3 % 3) * 64
        cs[base:base + 64, (k % 3) * 64:(k % 3) * 64 + 64] = c
    hi, lo = split(cs[...])
    deep[:, 0:192] = hi
    deep[:, 192:384] = hi
    deep[:, 384:576] = lo
    rowabs = jnp.sum(rowabs, axis=1, keepdims=True) + 0.5
    mask = [occupied[c // 2, c % 2:c % 2 + 1, :].astype(F32) for c in range(4)]
    has = {
        ("x", 0): slab > 0, ("x", 3): slab < n_slab - 1,
        ("y", 0): grp > 0, ("y", 3): grp < n_grp - 1,
    }

    for fx in range(4):
        for fy in range(4):
            sides = [has[k] for k in (("x", fx), ("y", fy)) if k in has]
            if sides:
                @pl.when(jnp.logical_not(functools.reduce(jnp.logical_and, sides)))
                def _():
                    for t in range(ITERS):
                        halo_in[t, fx * 4 + fy] = jnp.zeros((64, 256), F32)

    everyone = pl.ds(0, devs - 1)
    pltpu.make_async_copy(recv.at[everyone], recv.at[everyone], a2a_recv).wait()
    pltpu.make_async_copy(send.at[everyone], send.at[everyone], a2a_send).wait()

    for k in range(groups):
        tiles = recv[k * per:(k + 1) * per, 0:cap, :].reshape(128, 128)
        hi, lo = split(tiles)
        weights[k * 128:(k + 1) * 128, 0:128] = hi
        weights[k * 128:(k + 1) * 128, 128:256] = lo
    bits = cap.bit_length() - 1
    lanes = jnp.right_shift(lax.broadcasted_iota(jnp.int32, (devs, 128), 1), bits)
    source = jnp.bitwise_and(lax.broadcasted_iota(jnp.int32, (devs, 128), 0), per - 1)
    names = jnp.where(lanes == lax.rem(me, per), recv[:, cap, :], 0.0)
    shift = cap
    while shift < 128:
        names = names + pltpu.roll(names, shift, 1)
        shift *= 2
    names = jnp.where(lanes == source, names, 0.0)
    ids = [jnp.sum(names[k * per:(k + 1) * per], axis=0, keepdims=True) for k in range(groups)]
    ids = jnp.concatenate(ids, axis=1).astype(jnp.int32)
    lane = lax.broadcasted_iota(jnp.int32, (64, 256), 1)

    def frame(fx, fy, m):
        up = jnp.where(lane == 0, 0.0, pltpu.roll(m, 1, 1))
        down = jnp.where(lane == 255, 0.0, pltpu.roll(m, 255, 1))
        hi, lo = split(jnp.concatenate([up, m, down], axis=0))
        xs = [x for x in range(2) if 0 <= fx - x <= 2]
        ys = [y for y in range(2) if 0 <= fy - y <= 2]
        size = 64 * len(ys)
        starts = [(2 - (fx - x)) * 192 + (2 - (fy - ys[0])) * 64 for x in xs]
        left = jnp.concatenate([deep[s:s + size, :] for s in starts], axis=0)
        sums = jnp.dot(left, jnp.concatenate([hi, lo, hi], axis=0), preferred_element_type=F32)
        for a, x in enumerate(xs):
            for b, y in enumerate(ys):
                at = a * size + b * 64
                image[2 * x + y] += sums[at:at + 64]

    def both(a, b):
        return jnp.logical_and(a, b)

    def send_copy(t, src, f, dev):
        return pltpu.make_async_remote_copy(
            src_ref=src, dst_ref=halo_in.at[t, f], send_sem=halo_send.at[t, f],
            recv_sem=halo_recv.at[t, f], device_id=dev, device_id_type=MESH)

    def column_sends(t, c):
        x, y = c // 2, c % 2
        ref = halo_out.at[t, c]
        along_x = (slab + 1, grp) if x == 1 else (slab - 1, grp)
        along_y = (slab, grp + 1) if y == 1 else (slab, grp - 1)
        fx, fy = (0, 3)[x == 0], (0, 3)[y == 0]
        return [(has["x", 3 - fx], ref, fx * 4 + 1 + y, along_x),
                (has["y", 3 - fy], ref, (1 + x) * 4 + fy, along_y)]

    def corner_send(t, fx, y):
        f = fx * 4 + 1 + y
        corner = fx * 4 + (0 if y == 1 else 3)
        dev = (slab, grp + 1) if y == 1 else (slab, grp - 1)
        cond = both(has["x", fx], has["y", 3 if y == 1 else 0])
        return cond, halo_in.at[t, f], corner, dev

    def start(t, cond, ref, f, dev):
        @pl.when(cond)
        def _():
            send_copy(t, ref, f, dev).start()

    def arrived(t, cond, f):
        @pl.when(cond)
        def _():
            send_copy(t, halo_in.at[t, f], f, (slab, grp)).wait_recv()

    def offer(t, c, value):
        halo_out[t, c] = mask[c] * value
        for send_one in column_sends(t, c):
            start(t, *send_one)

    def apply(t, src, dst):
        for c in range(4):
            image[c] = jnp.zeros((64, 256), F32)
        for c in range(4):
            frame(1 + c // 2, 1 + c % 2, halo_out[t, c])
        for y in (0, 1):
            for fx in (0, 3):
                arrived(t, has["x", fx], fx * 4 + 1 + y)
                start(t, *corner_send(t, fx, y))
            for x in (0, 1):
                arrived(t, has["y", 3 * y], (1 + x) * 4 + 3 * y)
            for x in (0, 1):
                frame(1 + x, 3 * y, halo_in[t, (1 + x) * 4 + 3 * y])
        for fx in (0, 3):
            for y in (0, 1):
                frame(fx, 1 + y, halo_in[t, fx * 4 + 1 + y])
        for fx in (0, 3):
            for fy in (0, 3):
                arrived(t, both(has["x", fx], has["y", fy]), fx * 4 + fy)
        for fx in (0, 3):
            for fy in (0, 3):
                frame(fx, fy, halo_in[t, fx * 4 + fy])
        for c in range(4):
            dst[c] = diag[c] * src[c] - mask[c] * image[c]
        for c in range(4):
            for cond, ref, f, dev in column_sends(t, c):
                @pl.when(cond)
                def _():
                    send_copy(t, ref, f, dev).wait_send()
        for fx in (0, 3):
            for y in (0, 1):
                cond, ref, f, dev = corner_send(t, fx, y)

                @pl.when(cond)
                def _():
                    send_copy(t, ref, f, dev).wait_send()

    def start_sum(t, pairs):
        for k, (a, b) in enumerate(pairs):
            acc = a[0] * b[0]
            for c in range(1, 4):
                acc = acc + a[c] * b[c]
            part[t, k:k + 1, :] = jnp.broadcast_to(total(acc), (1, 128))
        parts[t, me] = part[t]

        def go(k, carry):
            other = lax.rem(me + k, devs)
            pltpu.make_async_remote_copy(
                src_ref=part.at[t], dst_ref=parts.at[t, me], send_sem=sum_send.at[t],
                recv_sem=sum_recv.at[t],
                device_id=(other // n_grp, lax.rem(other, n_grp)), device_id_type=MESH,
            ).start()
            return carry

        lax.fori_loop(1, devs, go, 0)

    def end_sum(t):
        ref = parts.at[t, everyone]
        pltpu.make_async_copy(ref, ref, sum_recv.at[t]).wait()
        pltpu.make_async_copy(ref, ref, sum_send.at[t]).wait()
        whole = jnp.sum(parts[t], axis=0)
        return whole[0:1, 0:1], whole[1:2, 0:1], whole[2:3, 0:1]

    for c in range(4):
        place = lax.broadcasted_iota(jnp.int32, (256, 1024), 0) + 256 * c
        hot = jnp.where(place == ids, 1.0, 0.0).astype(BF16)
        block = jnp.dot(hot, weights[...], preferred_element_type=F32)
        block = (block[:, 0:128] + block[:, 128:256]).T
        res[c] = block[0:64]
        offer(0, c, block[0:64])
        diag[c] = rowabs + 4.0 * block[64:128]

    apply(0, res, wvec)
    for c in range(4):
        offer(1, c, wvec[c])
    start_sum(0, [(res, res), (res, wvec)])
    apply(1, wvec, zvec)
    rr, dq, _ = end_sum(0)
    alpha = rr / dq
    for c in range(4):
        d = res[c]
        q = wvec[c]
        z = zvec[c]
        dvec[c] = d
        qvec[c] = q
        zq[c] = z
        x_out[c] = alpha * d
        res[c] = d - alpha * q
        w = q - alpha * z
        wvec[c] = w
        offer(2, c, w)
    start_sum(1, [(res, res), (res, wvec), (res, qvec)])
    apply(2, wvec, zvec)
    new, delta, eps = end_sum(1)
    beta = new / rr
    dq = delta + 2.0 * beta * eps + beta * beta * dq
    rr = new
    alpha = rr / dq
    for c in range(4):
        r = res[c]
        w = wvec[c]
        d = r + beta * dvec[c]
        q = w + beta * qvec[c]
        z = zvec[c] + beta * zq[c]
        dvec[c] = d
        qvec[c] = q
        x_out[c] = x_out[c] + alpha * d
        res[c] = r - alpha * q
        wvec[c] = w - alpha * z
    start_sum(2, [(res, res), (res, wvec), (res, qvec)])
    new, delta, eps = end_sum(2)
    beta = new / rr
    dq = delta + 2.0 * beta * eps + beta * beta * dq
    alpha = new / dq
    for c in range(4):
        r = res[c]
        d = r + beta * dvec[c]
        q = wvec[c] + beta * qvec[c]
        x_out[c] = x_out[c] + alpha * d
        r_out[c] = r - alpha * q


def on_device(samples, block_ids, tile_counts, occupied, coupling):
    n_slab, n_grp = lax.axis_size("slab"), lax.axis_size("grp")
    devs = n_slab * n_grp
    size_x, size_y, size_z = occupied.shape
    slots = samples.shape[0]
    cap = slots // devs
    columns = size_x * size_y
    vec = pltpu.VMEM((columns, 64, size_z), F32)
    vmem = pl.BlockSpec(memory_space=pltpu.VMEM)
    shape = jax.ShapeDtypeStruct((columns, 64, size_z), F32)
    x, r = pl.pallas_call(
        functools.partial(kernel, n_slab, n_grp),
        out_shape=(shape, shape),
        in_specs=[pl.BlockSpec(memory_space=pl.ANY)] * 5,
        out_specs=(vmem, vmem),
        scratch_shapes=[
            pltpu.VMEM((slots // 128, 1, 128), jnp.int32),
            pltpu.VMEM((slots // 128, 1, 128), jnp.int32),
            pltpu.VMEM(occupied.shape, jnp.int32),
            pltpu.VMEM(coupling.shape, F32),
            pltpu.VMEM((slots // 128, 6, 128, 128), F32),
            pltpu.VMEM((24, 128, 128), F32),
            pltpu.VMEM((128, 128), F32),
            pltpu.VMEM((devs, cap + 1, 128), F32),
            pltpu.VMEM((devs, cap + 1, 128), F32),
            pltpu.VMEM((576, 192), F32),
            pltpu.VMEM((576, 576), BF16),
            vec,
            pltpu.VMEM((ITERS, 4, 64, size_z), F32),
            pltpu.VMEM((ITERS, 16, 64, size_z), F32),
            vec, vec, vec, vec, vec, vec, vec,
            pltpu.VMEM((ITERS, 8, 128), F32),
            pltpu.VMEM((ITERS, devs, 8, 128), F32),
            pltpu.VMEM((slots, 256), BF16),
            pltpu.SemaphoreType.DMA((slots // 128,)),
            pltpu.SemaphoreType.DMA,
            pltpu.SemaphoreType.DMA,
            pltpu.SemaphoreType.DMA((ITERS, 16)),
            pltpu.SemaphoreType.DMA((ITERS, 16)),
            pltpu.SemaphoreType.DMA((ITERS,)),
            pltpu.SemaphoreType.DMA((ITERS,)),
            pltpu.SemaphoreType.DMA((4,)),
        ],
        compiler_params=pltpu.CompilerParams(
            collective_id=0, has_side_effects=True, vmem_limit_bytes=60 * 1024 * 1024,
        ),
    )(samples.transpose(1, 0, 2), tile_counts.reshape(slots // 128, 1, 128),
      block_ids.reshape(slots // 128, 1, 128), occupied, coupling)

    def shaped(v):
        return v.transpose(1, 0, 2).reshape(64, size_x, size_y, size_z)

    return shaped(x), shaped(r)


def solution(mesh):
    placed = (
        P(("slab", "grp"), None, None),
        P(("slab", "grp")),
        P(("slab", "grp")),
        P("slab", "grp", None),
        P(),
    )
    return jax.shard_map(
        on_device,
        mesh=mesh,
        in_specs=placed,
        out_specs=(P(None, "slab", "grp", None), P(None, "slab", "grp", None)),
        check_vma=False,
    )
```

```python
import functools

import jax
import jax.numpy as jnp
from jax import lax
from jax.experimental import pallas as pl
from jax.experimental.pallas import tpu as pltpu
from jax.sharding import PartitionSpec as P

ITERS = 3
MESH = pl.DeviceIdType.MESH
F32 = jnp.float32
BF16 = jnp.bfloat16


def hats(u):
    hat, low = [], []
    for j in range(5):
        g = u - float(j)
        h = jnp.maximum(1.0 - jnp.abs(g), 0.0)
        hat.append(h)
        low.append((0.5 + 0.5 * g) * h)
    values = [low[i] + (hat[i + 1] - low[i + 1]) for i in range(4)]
    slopes = [hat[i] - hat[i + 1] for i in range(4)]
    return values, slopes


def fold(rows):
    place = lax.broadcasted_iota(jnp.int32, (8, 128), 0)
    step = 1
    while len(rows) > 1:
        keep = jnp.bitwise_and(place, step) == 0
        rows = [
            jnp.where(keep, a, b) + pltpu.roll(jnp.where(keep, b, a), 8 - step, 0)
            for a, b in zip(rows[0::2], rows[1::2])
        ]
        step *= 2
    return rows[0]


def split(x):
    hi = x.astype(BF16)
    return hi, (x - hi.astype(F32)).astype(BF16)


def total(x):
    return jnp.sum(jnp.sum(x, axis=0, keepdims=True), axis=1, keepdims=True)


def kernel(n_slab, n_grp, samples, *refs):
    (count_in, name_in, occupied_in, coupling_in, x_out, r_out, counts, block_ids, occupied,
     coupling, held, fac, nodes, send, recv, cs, deep, diag, halo_out, halo_in, image, res, wvec,
     zvec, dvec, qvec, zq, part, parts, weights, held_sem, a2a_send, a2a_recv, halo_send, halo_recv,
     sum_send, sum_recv, in_sem) = refs
    devs = n_slab * n_grp
    cap = send.shape[1] - 1
    per = 128 // cap
    groups = samples.shape[1] // 128
    share = groups // n_slab
    size_x, size_y, size_z = occupied.shape
    bits_z = size_z.bit_length() - 1
    bits_y = (size_y * n_grp).bit_length() - 1
    slab = lax.axis_index("slab")
    grp = lax.axis_index("grp")
    me = slab * n_grp + grp

    def group_of(step):
        k = step // share
        away = jnp.where(k < n_slab // 2, k + n_slab // 2, n_slab - 1 - k)
        return lax.rem(slab + away, n_slab) * share + lax.rem(step, share)

    def fetch(g):
        rows = pl.ds(pl.multiple_of(g * 128, 128), 128)
        return pltpu.make_async_copy(samples.at[:, rows, :], held.at[g], held_sem.at[g])

    small = [(count_in, counts), (name_in, block_ids), (occupied_in, occupied),
             (coupling_in, coupling)]
    small = [pltpu.make_async_copy(a, b, in_sem.at[k]) for k, (a, b) in enumerate(small)]
    small[0].start()
    small[1].start()
    for step in range(groups):
        fetch(group_of(step)).start()
    small[2].start()
    small[3].start()
    barrier = pltpu.get_barrier_semaphore()

    def greet(k, carry):
        other = lax.rem(me + k, devs)
        pl.semaphore_signal(barrier, inc=1, device_id=(other // n_grp, lax.rem(other, n_grp)),
                            device_id_type=MESH)
        return carry

    lax.fori_loop(1, devs, greet, 0)

    small[0].wait()
    small[1].wait()

    def splat(step, carry):
        g = group_of(step)
        fetch(g).wait()
        name = block_ids[g]
        z = jnp.bitwise_and(name, size_z - 1)
        y = jnp.bitwise_and(jnp.right_shift(name, bits_z), size_y - 1)
        x = jnp.bitwise_and(jnp.right_shift(name, bits_z + bits_y), size_x - 1)
        name = ((x * size_y + y) * size_z + z).astype(F32)
        live = lax.broadcasted_iota(jnp.int32, (128, 128), 0) < counts[g]
        for d in range(3):
            values, slopes = hats(4.0 * held[g, d].T)
            normal = 4.0 * held[g, 3 + d].T
            if d == 0:
                normal = jnp.where(live, normal, 0.0)
            for i in range(4):
                fac[8 * d + i] = jnp.where(live, values[i], 0.0) if d == 0 else values[i]
                fac[8 * d + 4 + i] = slopes[i] * normal

        def pair(k, carry):
            i = k // 2
            first = lax.rem(k, 2) * 2

            def add(s, accs):
                at = pl.ds(pl.multiple_of(s * 8, 8), 8)
                v0 = fac[i, at, :]
                s0 = fac[4 + i, at, :]
                v2 = [fac[16 + l, at, :] for l in range(4)]
                s2 = [fac[20 + l, at, :] for l in range(4)]
                rhs, dens = [], []
                for e in range(2):
                    v1 = fac[8 + first + e, at, :]
                    s1 = fac[12 + first + e, at, :]
                    p = v0 * v1
                    q = s0 * v1 + v0 * s1
                    for l in range(4):
                        rhs.append(accs[4 * e + l] + (v2[l] * q + s2[l] * p))
                        dens.append(accs[8 + 4 * e + l] + v2[l] * p)
                return tuple(rhs + dens)

            zero = jnp.zeros((8, 128), F32)
            accs = lax.fori_loop(0, 16, add, (zero,) * 16, unroll=True)
            base = pl.multiple_of(8 * k, 8)
            nodes[pl.ds(base, 8), :] = fold(accs[0:8])
            nodes[pl.ds(64 + base, 8), :] = fold(accs[8:16])
            return carry

        lax.fori_loop(0, 8, pair, 0, unroll=True)
        tiles = nodes[...].T

        @pl.when(step == 0)
        def _():
            pl.semaphore_wait(barrier, devs - 1)

        for c in range(per):
            target = g * per + c
            send[target, 0:cap, :] = tiles[c * cap:(c + 1) * cap]
            send[target, cap:cap + 1, :] = name

            @pl.when(target != me)
            def _():
                pltpu.make_async_remote_copy(
                    src_ref=send.at[target], dst_ref=recv.at[me],
                    send_sem=a2a_send, recv_sem=a2a_recv,
                    device_id=(target // n_grp, lax.rem(target, n_grp)), device_id_type=MESH,
                ).start()

            @pl.when(target == me)
            def _():
                recv[target] = send[target]
        return carry

    lax.fori_loop(0, groups, splat, 0)

    small[2].wait()
    small[3].wait()

    rowabs = jnp.zeros((64, 64), F32)
    for k in range(27):
        c = 0.5 * (coupling[k] + coupling[26 - k].T)
        rowabs = rowabs + jnp.abs(c)
        base = (2 - k // 9) * 192 + (2 - k // 3 % 3) * 64
        cs[base:base + 64, (k % 3) * 64:(k % 3) * 64 + 64] = c
    hi, lo = split(cs[...])
    deep[:, 0:192] = hi
    deep[:, 192:384] = hi
    deep[:, 384:576] = lo
    rowabs = jnp.sum(rowabs, axis=1, keepdims=True) + 0.5
    mask = [occupied[c // 2, c % 2:c % 2 + 1, :].astype(F32) for c in range(4)]
    has = {
        ("x", 0): slab > 0, ("x", 3): slab < n_slab - 1,
        ("y", 0): grp > 0, ("y", 3): grp < n_grp - 1,
    }

    for fx in range(4):
        for fy in range(4):
            sides = [has[k] for k in (("x", fx), ("y", fy)) if k in has]
            if sides:
                @pl.when(jnp.logical_not(functools.reduce(jnp.logical_and, sides)))
                def _():
                    for t in range(ITERS):
                        halo_in[t, fx * 4 + fy] = jnp.zeros((64, 256), F32)

    everyone = pl.ds(0, devs - 1)
    pltpu.make_async_copy(recv.at[everyone], recv.at[everyone], a2a_recv).wait()
    pltpu.make_async_copy(send.at[everyone], send.at[everyone], a2a_send).wait()

    for k in range(groups):
        tiles = recv[k * per:(k + 1) * per, 0:cap, :].reshape(128, 128)
        hi, lo = split(tiles)
        weights[k * 128:(k + 1) * 128, 0:128] = hi
        weights[k * 128:(k + 1) * 128, 128:256] = lo
    bits = cap.bit_length() - 1
    lanes = jnp.right_shift(lax.broadcasted_iota(jnp.int32, (devs, 128), 1), bits)
    source = jnp.bitwise_and(lax.broadcasted_iota(jnp.int32, (devs, 128), 0), per - 1)
    names = jnp.where(lanes == lax.rem(me, per), recv[:, cap, :], 0.0)
    shift = cap
    while shift < 128:
        names = names + pltpu.roll(names, shift, 1)
        shift *= 2
    names = jnp.where(lanes == source, names, 0.0)
    ids = [jnp.sum(names[k * per:(k + 1) * per], axis=0, keepdims=True) for k in range(groups)]
    ids = jnp.concatenate(ids, axis=1).astype(jnp.int32)
    lane = lax.broadcasted_iota(jnp.int32, (64, 256), 1)

    def frame(fx, fy, m):
        up = jnp.where(lane == 0, 0.0, pltpu.roll(m, 1, 1))
        down = jnp.where(lane == 255, 0.0, pltpu.roll(m, 255, 1))
        hi, lo = split(jnp.concatenate([up, m, down], axis=0))
        xs = [x for x in range(2) if 0 <= fx - x <= 2]
        ys = [y for y in range(2) if 0 <= fy - y <= 2]
        size = 64 * len(ys)
        starts = [(2 - (fx - x)) * 192 + (2 - (fy - ys[0])) * 64 for x in xs]
        left = jnp.concatenate([deep[s:s + size, :] for s in starts], axis=0)
        sums = jnp.dot(left, jnp.concatenate([hi, lo, hi], axis=0), preferred_element_type=F32)
        for a, x in enumerate(xs):
            for b, y in enumerate(ys):
                at = a * size + b * 64
                image[2 * x + y] += sums[at:at + 64]

    def both(a, b):
        return jnp.logical_and(a, b)

    def send_copy(t, src, f, dev):
        return pltpu.make_async_remote_copy(
            src_ref=src, dst_ref=halo_in.at[t, f], send_sem=halo_send.at[t, f],
            recv_sem=halo_recv.at[t, f], device_id=dev, device_id_type=MESH)

    def column_sends(t, c):
        x, y = c // 2, c % 2
        ref = halo_out.at[t, c]
        along_x = (slab + 1, grp) if x == 1 else (slab - 1, grp)
        along_y = (slab, grp + 1) if y == 1 else (slab, grp - 1)
        fx, fy = (0, 3)[x == 0], (0, 3)[y == 0]
        return [(has["x", 3 - fx], ref, fx * 4 + 1 + y, along_x),
                (has["y", 3 - fy], ref, (1 + x) * 4 + fy, along_y)]

    def corner_send(t, fx, y):
        f = fx * 4 + 1 + y
        corner = fx * 4 + (0 if y == 1 else 3)
        dev = (slab, grp + 1) if y == 1 else (slab, grp - 1)
        cond = both(has["x", fx], has["y", 3 if y == 1 else 0])
        return cond, halo_in.at[t, f], corner, dev

    def start(t, cond, ref, f, dev):
        @pl.when(cond)
        def _():
            send_copy(t, ref, f, dev).start()

    def arrived(t, cond, f):
        @pl.when(cond)
        def _():
            send_copy(t, halo_in.at[t, f], f, (slab, grp)).wait_recv()

    def offer(t, c, value):
        halo_out[t, c] = mask[c] * value
        for send_one in column_sends(t, c):
            start(t, *send_one)

    def apply(t, src, dst):
        for c in range(4):
            image[c] = jnp.zeros((64, 256), F32)
        for c in range(4):
            frame(1 + c // 2, 1 + c % 2, halo_out[t, c])
        for y in (0, 1):
            for fx in (0, 3):
                arrived(t, has["x", fx], fx * 4 + 1 + y)
                start(t, *corner_send(t, fx, y))
            for x in (0, 1):
                arrived(t, has["y", 3 * y], (1 + x) * 4 + 3 * y)
            for x in (0, 1):
                frame(1 + x, 3 * y, halo_in[t, (1 + x) * 4 + 3 * y])
        for fx in (0, 3):
            for y in (0, 1):
                frame(fx, 1 + y, halo_in[t, fx * 4 + 1 + y])
        for fx in (0, 3):
            for fy in (0, 3):
                arrived(t, both(has["x", fx], has["y", fy]), fx * 4 + fy)
        for fx in (0, 3):
            for fy in (0, 3):
                frame(fx, fy, halo_in[t, fx * 4 + fy])
        for c in range(4):
            dst[c] = diag[c] * src[c] - mask[c] * image[c]
        for c in range(4):
            for cond, ref, f, dev in column_sends(t, c):
                @pl.when(cond)
                def _():
                    send_copy(t, ref, f, dev).wait_send()
        for fx in (0, 3):
            for y in (0, 1):
                cond, ref, f, dev = corner_send(t, fx, y)

                @pl.when(cond)
                def _():
                    send_copy(t, ref, f, dev).wait_send()

    def start_sum(t, pairs):
        row = jnp.zeros((1, 128), F32)
        column = lax.broadcasted_iota(jnp.int32, (1, 128), 1)
        for k, (a, b) in enumerate(pairs):
            acc = a[0] * b[0]
            for c in range(1, 4):
                acc = acc + a[c] * b[c]
            row = jnp.where(column == k, total(acc), row)
        part[t] = row
        parts[t, me] = row

        def go(k, carry):
            other = lax.rem(me + k, devs)
            pltpu.make_async_remote_copy(
                src_ref=part.at[t], dst_ref=parts.at[t, me], send_sem=sum_send.at[t],
                recv_sem=sum_recv.at[t],
                device_id=(other // n_grp, lax.rem(other, n_grp)), device_id_type=MESH,
            ).start()
            return carry

        lax.fori_loop(1, devs, go, 0)

    def end_sum(t):
        ref = parts.at[t, everyone]
        pltpu.make_async_copy(ref, ref, sum_recv.at[t]).wait()
        pltpu.make_async_copy(ref, ref, sum_send.at[t]).wait()
        whole = jnp.sum(parts[t], axis=0)
        return whole[:, 0:1], whole[:, 1:2], whole[:, 2:3]

    for c in range(4):
        place = lax.broadcasted_iota(jnp.int32, (256, 1024), 0) + 256 * c
        hot = jnp.where(place == ids, 1.0, 0.0).astype(BF16)
        block = jnp.dot(hot, weights[...], preferred_element_type=F32)
        block = (block[:, 0:128] + block[:, 128:256]).T
        res[c] = block[0:64]
        offer(0, c, block[0:64])
        diag[c] = rowabs + 4.0 * block[64:128]

    apply(0, res, wvec)
    for c in range(4):
        offer(1, c, wvec[c])
    start_sum(0, [(res, res), (res, wvec)])
    apply(1, wvec, zvec)
    rr, dq, _ = end_sum(0)
    alpha = rr / dq
    for c in range(4):
        d = res[c]
        q = wvec[c]
        z = zvec[c]
        dvec[c] = d
        qvec[c] = q
        zq[c] = z
        x_out[c] = alpha * d
        res[c] = d - alpha * q
        w = q - alpha * z
        wvec[c] = w
        offer(2, c, w)
    start_sum(1, [(res, res), (res, wvec), (res, qvec)])
    apply(2, wvec, zvec)
    new, delta, eps = end_sum(1)
    beta = new / rr
    dq = delta + 2.0 * beta * eps + beta * beta * dq
    rr = new
    alpha = rr / dq
    for c in range(4):
        r = res[c]
        w = wvec[c]
        d = r + beta * dvec[c]
        q = w + beta * qvec[c]
        z = zvec[c] + beta * zq[c]
        dvec[c] = d
        qvec[c] = q
        x_out[c] = x_out[c] + alpha * d
        res[c] = r - alpha * q
        wvec[c] = w - alpha * z
    start_sum(2, [(res, res), (res, wvec), (res, qvec)])
    new, delta, eps = end_sum(2)
    beta = new / rr
    dq = delta + 2.0 * beta * eps + beta * beta * dq
    alpha = new / dq
    for c in range(4):
        r = res[c]
        d = r + beta * dvec[c]
        q = wvec[c] + beta * qvec[c]
        x_out[c] = x_out[c] + alpha * d
        r_out[c] = r - alpha * q


def on_device(samples, block_ids, tile_counts, occupied, coupling):
    n_slab, n_grp = lax.axis_size("slab"), lax.axis_size("grp")
    devs = n_slab * n_grp
    size_x, size_y, size_z = occupied.shape
    slots = samples.shape[0]
    cap = slots // devs
    columns = size_x * size_y
    vec = pltpu.VMEM((columns, 64, size_z), F32)
    vmem = pl.BlockSpec(memory_space=pltpu.VMEM)
    shape = jax.ShapeDtypeStruct((columns, 64, size_z), F32)
    x, r = pl.pallas_call(
        functools.partial(kernel, n_slab, n_grp),
        out_shape=(shape, shape),
        in_specs=[pl.BlockSpec(memory_space=pl.ANY)] * 5,
        out_specs=(vmem, vmem),
        scratch_shapes=[
            pltpu.VMEM((slots // 128, 1, 128), jnp.int32),
            pltpu.VMEM((slots // 128, 1, 128), jnp.int32),
            pltpu.VMEM(occupied.shape, jnp.int32),
            pltpu.VMEM(coupling.shape, F32),
            pltpu.VMEM((slots // 128, 6, 128, 128), F32),
            pltpu.VMEM((24, 128, 128), F32),
            pltpu.VMEM((128, 128), F32),
            pltpu.VMEM((devs, cap + 1, 128), F32),
            pltpu.VMEM((devs, cap + 1, 128), F32),
            pltpu.VMEM((576, 192), F32),
            pltpu.VMEM((576, 576), BF16),
            vec,
            pltpu.VMEM((ITERS, 4, 64, size_z), F32),
            pltpu.VMEM((ITERS, 16, 64, size_z), F32),
            vec, vec, vec, vec, vec, vec, vec,
            pltpu.VMEM((ITERS, 1, 128), F32),
            pltpu.VMEM((ITERS, devs, 1, 128), F32),
            pltpu.VMEM((slots, 256), BF16),
            pltpu.SemaphoreType.DMA((slots // 128,)),
            pltpu.SemaphoreType.DMA,
            pltpu.SemaphoreType.DMA,
            pltpu.SemaphoreType.DMA((ITERS, 16)),
            pltpu.SemaphoreType.DMA((ITERS, 16)),
            pltpu.SemaphoreType.DMA((ITERS,)),
            pltpu.SemaphoreType.DMA((ITERS,)),
            pltpu.SemaphoreType.DMA((4,)),
        ],
        compiler_params=pltpu.CompilerParams(
            collective_id=0, has_side_effects=True, vmem_limit_bytes=60 * 1024 * 1024,
        ),
    )(samples.transpose(1, 0, 2), tile_counts.reshape(slots // 128, 1, 128),
      block_ids.reshape(slots // 128, 1, 128), occupied, coupling)

    def shaped(v):
        return v.transpose(1, 0, 2).reshape(64, size_x, size_y, size_z)

    return shaped(x), shaped(r)


def solution(mesh):
    placed = (
        P(("slab", "grp"), None, None),
        P(("slab", "grp")),
        P(("slab", "grp")),
        P("slab", "grp", None),
        P(),
    )
    return jax.shard_map(
        on_device,
        mesh=mesh,
        in_specs=placed,
        out_specs=(P(None, "slab", "grp", None), P(None, "slab", "grp", None)),
        check_vma=False,
    )
```
